32 devices in a mesh: tm: 2 (over y), chan: 16 (over z, x, core).
Axes of the slice: x: 2, y: 2, z: 4, core: 2. Of those that a mesh axis runs over, the one named last changes fastest.
Arguments:
- record: bfloat16 [8192, 8192], P('chan', 'tm'), may hold values from -6 to 6
- fan_mask: int32 [256, 8192], P('chan'), may hold values 0 or 1
Outputs:
- filtered: float32 [8192, 8192], P('chan', 'tm')
The draws below stay inside these ranges and needn't reach their ends.
All inputs are finite; a program needn't handle non-finite values. No bound on the sum of `fan_mask` on one device may be relied on, other than what follows from the above.
Results may differ from the reference program's by a relative error of at most 0.0084.
Values may be sent and summed in bfloat16 or wider, within the bound.
A program may use at most 128 MiB of HBM per device.

```python
import math
import jax
import jax.numpy as jnp
from jax import lax

NCH = 8192
SECTION_A = 64
WIN = 512
SECTION_B = 128
HOP = 256
BINS = 256
FRAMES = 32
SAMPLES = 8192


def place_ends(entries, own_key, smallest, high):
    dims = entries.shape
    spot = [jax.random.randint(jax.random.fold_in(own_key, axis), (), 0, dims[axis]) for axis in range(len(dims))]
    entries = entries.at[tuple(spot)].set(smallest)
    longest = dims.index(max(dims))
    spot[longest] = (spot[longest] + 1) % dims[longest]
    return entries.at[tuple(spot)].set(high)


def levels(own_key, dims, split, low, top_value):
    loudness = 1.0
    for axis_at, shards_of in split:
        draws = jax.random.uniform(jax.random.fold_in(jax.random.fold_in(own_key, 6), axis_at), (shards_of,), jnp.float32, low / len(split), top_value / len(split))
        loudness = loudness * jnp.repeat(jnp.exp(draws), dims[axis_at] // shards_of).reshape((-1,) + (1,) * (len(dims) - 1 - axis_at))
    return loudness


def gaussian(own_key, dims, width, most, split=(), kind=jnp.bfloat16):
    entries = jax.random.normal(own_key, dims, jnp.float32) * width
    if len(split) > 0:
        entries = levels(own_key, dims, split, -0.22, 0.18) * entries
    return jnp.clip(entries, min=-most, max=most).astype(kind)


def setup_inputs(seed: int = 0) -> dict:
    key_list = jax.random.split(jax.random.key(seed), 3)
    record = gaussian(key_list[0], (NCH, SAMPLES), 1.0, 6.0, ((0, 16), (1, 2)))
    fan_mask = place_ends((jax.random.randint(key_list[1], (BINS, NCH), 0, 2) < 1).astype(jnp.int32), jax.random.fold_in(key_list[1], 1), 0, 1)
    return {"record": record, "fan_mask": fan_mask}


def hann_taper(length):
    steps = jnp.arange(length, dtype=jnp.int32).astype(jnp.float32)
    return 0.5 - 0.5 * jnp.cos(steps * (2.0 * math.pi / length))


def time_table(length, bins):
    rows = jnp.arange(length, dtype=jnp.int32)[:, None]
    cols = jnp.arange(bins, dtype=jnp.int32)[None, :]
    phase = ((rows * cols) % length).astype(jnp.float32) * (2.0 * math.pi / length)
    return jnp.concatenate([jnp.cos(phase), -jnp.sin(phase)], axis=1).astype(jnp.bfloat16)


def inverse_time_table(length, bins):
    rows = jnp.arange(bins, dtype=jnp.int32)[:, None]
    cols = jnp.arange(length, dtype=jnp.int32)[None, :]
    phase = ((rows * cols) % length).astype(jnp.float32) * (2.0 * math.pi / length)
    weight = jnp.where(rows == 0, 1.0, 2.0).astype(jnp.float32) / length
    return jnp.stack([weight * jnp.cos(phase), -weight * jnp.sin(phase)]).astype(jnp.bfloat16)


def block_table(order_len, exponent_sign):
    rows = jnp.arange(order_len, dtype=jnp.int32)[:, None]
    cols = jnp.arange(order_len, dtype=jnp.int32)[None, :]
    phase = ((rows * cols) % order_len).astype(jnp.float32) * (2.0 * math.pi / order_len)
    cosine = jnp.cos(phase)
    sine = exponent_sign * jnp.sin(phase)
    real_row = jnp.stack([cosine, sine], axis=1)
    imag_row = jnp.stack([-sine, cosine], axis=1)
    return jnp.stack([real_row, imag_row], axis=0).astype(jnp.bfloat16)


def twiddle_pair(row_count, col_count, total, exponent_sign):
    rows = jnp.arange(row_count, dtype=jnp.int32)[:, None]
    cols = jnp.arange(col_count, dtype=jnp.int32)[None, :]
    phase = ((rows * cols) % total).astype(jnp.float32) * (2.0 * math.pi / total)
    return jnp.cos(phase), exponent_sign * jnp.sin(phase)


def rotate(values, cosine, sine):
    return jnp.stack([values[0] * cosine - values[1] * sine, values[0] * sine + values[1] * cosine])


def wide_einsum(form, left, right):
    return jnp.einsum(form, left.astype(jnp.float32), right.astype(jnp.float32), precision=lax.Precision.HIGHEST)


def reference(record, fan_mask):
    taper = hann_taper(WIN)
    forward_time = time_table(WIN, BINS)
    inverse_time = inverse_time_table(WIN, BINS)
    outer_fwd = block_table(SECTION_A, -1.0)
    inner_fwd = block_table(SECTION_B, -1.0)
    inner_inv = block_table(SECTION_B, 1.0)
    outer_inv = block_table(SECTION_A, 1.0)
    fwd_cos, fwd_sin = twiddle_pair(SECTION_A, SECTION_B, NCH, -1.0)
    inv_cos, inv_sin = twiddle_pair(SECTION_A, SECTION_B, NCH, 1.0)
    fk_gate = fan_mask.reshape(BINS, SECTION_B, SECTION_A).transpose(0, 2, 1).astype(jnp.float32)
    padded = jnp.concatenate([record, jnp.zeros((NCH, HOP), record.dtype)], axis=1)

    def advance(previous, frame_index):
        frame_rows = lax.dynamic_slice_in_dim(padded, frame_index * HOP, WIN, 1)
        windowed = (frame_rows.astype(jnp.float32) * taper).astype(jnp.bfloat16)
        spectra = jnp.dot(windowed, forward_time, preferred_element_type=jnp.float32).astype(jnp.bfloat16)
        spectra = spectra.reshape(NCH, 2, BINS).transpose(1, 2, 0).reshape(2, BINS, SECTION_A, SECTION_B)
        section_one = wide_einsum('ikpq,ipoj->okjq', spectra, outer_fwd)
        section_one = rotate(section_one, fwd_cos, fwd_sin).astype(jnp.bfloat16)
        fk_plane = wide_einsum('ikjq,iqor->okjr', section_one, inner_fwd)
        fk_plane = (fk_plane * fk_gate[None]).astype(jnp.bfloat16)
        section_three = wide_einsum('ikjr,iroq->okjq', fk_plane, inner_inv)
        section_three = rotate(section_three, inv_cos, inv_sin).astype(jnp.bfloat16)
        restored = wide_einsum('ikjq,ijop->okpq', section_three, outer_inv) * (1.0 / NCH)
        restored = restored.astype(jnp.bfloat16).reshape(2, BINS, NCH)
        signal = wide_einsum('ikc,ikn->cn', restored, inverse_time)
        return signal[:, HOP:], signal[:, :HOP] + previous

    start = jnp.zeros((NCH, HOP), jnp.float32)
    _, output_blocks = lax.scan(advance, start, jnp.arange(FRAMES, dtype=jnp.int32))
    return output_blocks.transpose(1, 0, 2).reshape(NCH, SAMPLES)
```

```python
import functools
import math

import jax
import jax.numpy as jnp
from jax import lax
from jax.experimental import pallas as pl
from jax.experimental.pallas import tpu as pltpu
from jax.sharding import PartitionSpec as P

NCH = 8192
SECTION_A = 64
WIN = 512
SECTION_B = 128
HOP = 256
BINS = 256


def passed_along(value, axis, by):
    peers = lax.axis_size(axis)
    pairs = [(i, i + by) for i in range(peers) if 0 <= i + by < peers]
    return lax.ppermute(value, axis, pairs)


def hann_taper(length):
    steps = jnp.arange(length, dtype=jnp.int32).astype(jnp.float32)
    return 0.5 - 0.5 * jnp.cos(steps * (2.0 * math.pi / length))


def time_table(length, bins):
    rows = jnp.arange(length, dtype=jnp.int32)[:, None]
    cols = jnp.arange(bins, dtype=jnp.int32)[None, :]
    phase = (rows * cols % length).astype(jnp.float32) * (2.0 * math.pi / length)
    return jnp.concatenate([jnp.cos(phase), -jnp.sin(phase)], axis=1).astype(jnp.bfloat16)


def inverse_time_table(length, bins):
    rows = jnp.arange(bins, dtype=jnp.int32)[:, None]
    cols = jnp.arange(length, dtype=jnp.int32)[None, :]
    phase = (rows * cols % length).astype(jnp.float32) * (2.0 * math.pi / length)
    weight = jnp.where(rows == 0, 1.0, 2.0).astype(jnp.float32) / length
    return jnp.stack([weight * jnp.cos(phase), -weight * jnp.sin(phase)]).astype(jnp.bfloat16)


def block_table(order_len, exponent_sign):
    rows = jnp.arange(order_len, dtype=jnp.int32)[:, None]
    cols = jnp.arange(order_len, dtype=jnp.int32)[None, :]
    phase = (rows * cols % order_len).astype(jnp.float32) * (2.0 * math.pi / order_len)
    cosine = jnp.cos(phase)
    sine = exponent_sign * jnp.sin(phase)
    real_row = jnp.stack([cosine, sine], axis=1)
    imag_row = jnp.stack([-sine, cosine], axis=1)
    return jnp.stack([real_row, imag_row], axis=0).astype(jnp.bfloat16)


def twiddle_pair(row_count, col_count, total, exponent_sign):
    rows = jnp.arange(row_count, dtype=jnp.int32)[:, None]
    cols = jnp.arange(col_count, dtype=jnp.int32)[None, :]
    phase = (rows * cols % total).astype(jnp.float32) * (2.0 * math.pi / total)
    return (jnp.cos(phase), exponent_sign * jnp.sin(phase))


def rotate(values, cosine, sine):
    return jnp.stack([values[0] * cosine - values[1] * sine, values[0] * sine + values[1] * cosine])


def bins_body(record, fan_mask):
    channels, span_len = record.shape
    frames_here = span_len // HOP
    taper = hann_taper(WIN)
    forward_time = time_table(WIN, BINS).T
    inverse_time = inverse_time_table(WIN, BINS)
    outer_fwd = block_table(SECTION_A, -1.0)
    inner_fwd = block_table(SECTION_B, -1.0)
    inner_inv = block_table(SECTION_B, 1.0)
    outer_inv = block_table(SECTION_A, 1.0)
    fwd_cos, fwd_sin = twiddle_pair(SECTION_A, SECTION_B, NCH, -1.0)
    inv_cos, inv_sin = twiddle_pair(SECTION_A, SECTION_B, NCH, 1.0)
    fwd_cos = fwd_cos[:, None, None, :]
    fwd_sin = fwd_sin[:, None, None, :]
    inv_cos = inv_cos[:, None, None, :]
    inv_sin = inv_sin[:, None, None, :]
    local_bins = fan_mask.shape[0]
    fk_gate = (
        fan_mask.reshape(local_bins, SECTION_B, SECTION_A).transpose(2, 0, 1).astype(jnp.float32)
    )
    fk_gate = fk_gate[:, :, None, None, :]
    time_major = record.T
    rim_rows = passed_along(time_major[:HOP], "tm", -1)
    extended = jnp.concatenate([time_major, rim_rows], axis=0)
    blocks = extended.reshape(frames_here + 1, HOP, channels).astype(jnp.float32)
    first_half = (blocks[:-1] * taper[:HOP, None]).astype(jnp.bfloat16)
    second_half = (blocks[1:] * taper[HOP:, None]).astype(jnp.bfloat16)
    spectra = jnp.einsum(
        "jn,fnc->jfc", forward_time[:, :HOP], first_half, preferred_element_type=jnp.float32
    )
    spectra = spectra + jnp.einsum(
        "jn,fnc->jfc", forward_time[:, HOP:], second_half, preferred_element_type=jnp.float32
    )
    spectra = spectra.astype(jnp.bfloat16).reshape(2, BINS, frames_here, channels)
    bin_grid = lax.all_to_all(spectra, "chan", split_axis=1, concat_axis=3, tiled=True)
    bin_count = bin_grid.shape[1]
    item_count = bin_grid.shape[2]
    split_grid = bin_grid.reshape(2, bin_count, item_count, SECTION_A, SECTION_B)
    section_one = jnp.einsum(
        "ipoj,ikfpq->ojkfq", outer_fwd, split_grid, preferred_element_type=jnp.float32
    )
    section_one = rotate(section_one, fwd_cos, fwd_sin).astype(jnp.bfloat16)
    fk_plane = jnp.einsum(
        "ijkfq,iqor->jkfor", section_one, inner_fwd, preferred_element_type=jnp.float32
    )
    fk_plane = (fk_plane * fk_gate).astype(jnp.bfloat16)
    section_three = jnp.einsum(
        "jkfir,iroq->jkfoq", fk_plane, inner_inv, preferred_element_type=jnp.float32
    )
    real_part = section_three[:, :, :, 0]
    imag_part = section_three[:, :, :, 1]
    section_three = jnp.stack(
        [real_part * inv_cos - imag_part * inv_sin, real_part * inv_sin + imag_part * inv_cos]
    ).astype(jnp.bfloat16)
    restored = jnp.einsum(
        "ijkfq,ijop->opkfq", section_three, outer_inv, preferred_element_type=jnp.float32
    )
    restored = (restored * (1.0 / NCH)).astype(jnp.bfloat16)
    restored = restored.transpose(0, 2, 3, 1, 4).reshape(2, bin_count, item_count, NCH)
    returned = lax.all_to_all(restored, "chan", split_axis=3, concat_axis=1, tiled=True)
    signal = jnp.einsum("ikn,ikfc->nfc", inverse_time, returned, preferred_element_type=jnp.float32)
    head_half = signal[:HOP]
    tail_half = signal[HOP:]
    carried = passed_along(tail_half[:, -1].astype(jnp.bfloat16), "tm", 1).astype(jnp.float32)
    output_blocks = head_half + jnp.concatenate([carried[:, None], tail_half[:, :-1]], axis=1)
    return output_blocks.transpose(2, 1, 0).reshape(channels, span_len)


LANES = 128
GROUP = 4


def flat_table(order_len, exponent_sign):
    table = block_table(order_len, exponent_sign)
    return table.transpose(2, 3, 0, 1).reshape(2 * order_len, 2 * order_len)


def frame_kernel(
    first, second, taper, fwd_time, inv_time, w_one, w_two, w_three, w_four,
    tw_cos, tw_sin, gate, head, tail, by_q, by_j, restored,
):
    def rows_at(index, size):
        return pl.ds(pl.multiple_of(index * size, size), size)

    parts = fwd_time.shape[0]
    for part in range(parts):
        lanes = slice(part * LANES, (part + 1) * LANES)

        @pl.loop(0, SECTION_A // GROUP)
        def _(step):
            rows = rows_at(step, GROUP * SECTION_B)
            left = (first[rows, :].astype(jnp.float32) * taper[:, :HOP]).astype(jnp.bfloat16)
            right = (second[rows, :].astype(jnp.float32) * taper[:, HOP:]).astype(jnp.bfloat16)
            spectra = jnp.dot(left, fwd_time[part, :HOP], preferred_element_type=jnp.float32)
            spectra += jnp.dot(right, fwd_time[part, HOP:], preferred_element_type=jnp.float32)
            for g in range(GROUP):
                for i in range(2):
                    by_q[i, pl.ds(step * GROUP + g, SECTION_B, stride=SECTION_A), :] = spectra[
                        g * SECTION_B : (g + 1) * SECTION_B, i * LANES : (i + 1) * LANES
                    ]

        @pl.loop(0, SECTION_B // GROUP)
        def _(step):
            columns = []
            for g in range(GROUP):
                rows = rows_at(step * GROUP + g, SECTION_A)
                columns.append(
                    jnp.concatenate([by_q[0, rows, :], by_q[1, rows, :]], axis=0).astype(jnp.bfloat16)
                )
            total = jnp.dot(
                w_one[...], jnp.concatenate(columns, axis=1), preferred_element_type=jnp.float32
            )
            for g in range(GROUP):
                rows = rows_at(step * GROUP + g, SECTION_A)
                cosine, sine = tw_cos[rows, :], tw_sin[rows, :]
                real = total[:SECTION_A, g * LANES : (g + 1) * LANES]
                imag = total[SECTION_A:, g * LANES : (g + 1) * LANES]
                spread = pl.ds(step * GROUP + g, SECTION_A, stride=SECTION_B)
                by_j[0, spread, :] = real * cosine + imag * sine
                by_j[1, spread, :] = imag * cosine - real * sine

        @pl.loop(0, SECTION_A // GROUP)
        def _(step):
            columns, gates = [], []
            for g in range(GROUP):
                rows = rows_at(step * GROUP + g, SECTION_B)
                columns.append(
                    jnp.concatenate([by_j[0, rows, :], by_j[1, rows, :]], axis=0).astype(jnp.bfloat16)
                )
                gates.append(gate[rows, lanes].astype(jnp.float32))
            plane = jnp.dot(
                w_two[...], jnp.concatenate(columns, axis=1), preferred_element_type=jnp.float32
            )
            passing = jnp.concatenate(gates, axis=1)
            plane = plane * jnp.concatenate([passing, passing], axis=0)
            total = jnp.dot(
                w_three[...], plane.astype(jnp.bfloat16), preferred_element_type=jnp.float32
            )
            for g in range(GROUP):
                spread = pl.ds(step * GROUP + g, SECTION_B, stride=SECTION_A)
                for i in range(2):
                    by_q[i, spread, :] = total[
                        i * SECTION_B : (i + 1) * SECTION_B, g * LANES : (g + 1) * LANES
                    ]

        @pl.loop(0, SECTION_B // GROUP)
        def _(step):
            columns = []
            for g in range(GROUP):
                rows = rows_at(step * GROUP + g, SECTION_A)
                cosine, sine = tw_cos[rows, :], tw_sin[rows, :]
                real, imag = by_q[0, rows, :], by_q[1, rows, :]
                columns.append(
                    jnp.concatenate(
                        [real * cosine - imag * sine, real * sine + imag * cosine], axis=0
                    ).astype(jnp.bfloat16)
                )
            total = jnp.dot(
                w_four[...], jnp.concatenate(columns, axis=1), preferred_element_type=jnp.float32
            ) * (1.0 / NCH)
            for g in range(GROUP):
                spread = pl.ds(step * GROUP + g, SECTION_A, stride=SECTION_B)
                for i in range(2):
                    by_j[i, spread, :] = total[
                        i * SECTION_A : (i + 1) * SECTION_A, g * LANES : (g + 1) * LANES
                    ]

        @pl.loop(0, SECTION_A // GROUP)
        def _(step):
            rows = rows_at(step, GROUP * SECTION_B)
            for i in range(2):
                at = (2 * part + i) * LANES
                restored[rows, at : at + LANES] = by_j[i, rows, :].astype(jnp.bfloat16)

    @pl.loop(0, SECTION_A // GROUP)
    def _(step):
        rows = rows_at(step, GROUP * SECTION_B)
        signal = jnp.dot(restored[rows, :], inv_time[...], preferred_element_type=jnp.float32)
        head[rows, :] = signal[:, :HOP].astype(head.dtype)
        tail[rows, :] = signal[:, HOP:].astype(tail.dtype)


def frame_tables():
    parts = BINS // LANES
    fwd_time = time_table(WIN, BINS).reshape(WIN, 2, parts, LANES)
    fwd_time = fwd_time.transpose(2, 0, 1, 3).reshape(parts, WIN, 2 * LANES)
    inv_time = inverse_time_table(WIN, BINS).reshape(2, parts, LANES, WIN)
    inv_time = inv_time.transpose(1, 0, 2, 3).reshape(2 * BINS, WIN)
    tw_cos, tw_sin = twiddle_pair(SECTION_B, SECTION_A, NCH, 1.0)
    spread = (SECTION_B, SECTION_A, LANES)
    return (
        hann_taper(WIN)[None, :],
        fwd_time,
        inv_time,
        flat_table(SECTION_A, -1.0),
        flat_table(SECTION_B, -1.0),
        flat_table(SECTION_B, 1.0),
        flat_table(SECTION_A, 1.0),
        jnp.broadcast_to(tw_cos[:, :, None], spread).reshape(NCH, LANES),
        jnp.broadcast_to(tw_sin[:, :, None], spread).reshape(NCH, LANES),
    )


def filter_frame(first, second, tables, gate):
    half = jax.ShapeDtypeStruct((NCH, HOP), jnp.bfloat16)
    whole = pl.BlockSpec(memory_space=pltpu.VMEM)
    return pl.pallas_call(
        frame_kernel,
        out_shape=(half, half),
        in_specs=[whole] * (3 + len(tables)),
        out_specs=(whole, whole),
        scratch_shapes=[
            pltpu.VMEM((2, NCH, LANES), jnp.float32),
            pltpu.VMEM((2, NCH, LANES), jnp.float32),
            pltpu.VMEM((NCH, 2 * BINS), jnp.bfloat16),
        ],
        compiler_params=pltpu.CompilerParams(vmem_limit_bytes=60 * 1024 * 1024),
        cost_estimate=pl.CostEstimate(
            flops=16_000_000_000, bytes_accessed=30_000_000, transcendentals=0
        ),
    )(first, second, *tables, gate)


def shifted(value, by):
    axes = ("tm", "chan")
    peers = lax.axis_size("tm") * lax.axis_size("chan")
    pairs = [(i, i + by) for i in range(peers) if 0 <= i + by < peers]
    return lax.ppermute(value, axes, pairs)


def frames_body(record, fan_mask):
    channels, span_len = record.shape
    local_bins = fan_mask.shape[0]
    gate = fan_mask.astype(jnp.bfloat16).reshape(local_bins, SECTION_B, SECTION_A)
    gate = gate.transpose(0, 2, 1).reshape(local_bins, NCH)
    gate = lax.all_gather(gate, "chan", axis=0, tiled=True).T
    tables = frame_tables()
    mine = lax.all_to_all(record, "chan", split_axis=1, concat_axis=0, tiled=True)
    after = shifted(mine[:, :HOP], -1)
    held = mine.shape[1] // HOP
    blocks = [mine[:, f * HOP : (f + 1) * HOP] for f in range(held)] + [after]
    halves = [filter_frame(blocks[f], blocks[f + 1], tables, gate) for f in range(held)]
    before = shifted(halves[-1][1], 1)
    tails = [before] + [halves[f][1] for f in range(held - 1)]
    sums = [
        (halves[f][0].astype(jnp.float32) + tails[f].astype(jnp.float32)).astype(jnp.bfloat16)
        for f in range(held)
    ]
    result = sums[0] if held == 1 else jnp.concatenate(sums, axis=1)
    result = lax.all_to_all(result, "chan", split_axis=0, concat_axis=1, tiled=True)
    return result.astype(jnp.float32)


def body(record, fan_mask):
    if (record.shape[1] // HOP) % lax.axis_size("chan") == 0:
        return frames_body(record, fan_mask)
    return bins_body(record, fan_mask)


def solution(mesh):
    placed = (P("chan", "tm"), P("chan", None))
    return jax.shard_map(
        body, mesh=mesh, in_specs=placed, out_specs=P("chan", "tm"), check_vma=False
    )
```

```python
import functools
import math

import jax
import jax.numpy as jnp
from jax import lax
from jax.experimental import pallas as pl
from jax.experimental.pallas import tpu as pltpu
from jax.sharding import PartitionSpec as P

NCH = 8192
SECTION_A = 64
WIN = 512
SECTION_B = 128
HOP = 256
BINS = 256


def passed_along(value, axis, by):
    peers = lax.axis_size(axis)
    pairs = [(i, i + by) for i in range(peers) if 0 <= i + by < peers]
    return lax.ppermute(value, axis, pairs)


def hann_taper(length):
    steps = jnp.arange(length, dtype=jnp.int32).astype(jnp.float32)
    return 0.5 - 0.5 * jnp.cos(steps * (2.0 * math.pi / length))


def time_table(length, bins):
    rows = jnp.arange(length, dtype=jnp.int32)[:, None]
    cols = jnp.arange(bins, dtype=jnp.int32)[None, :]
    phase = (rows * cols % length).astype(jnp.float32) * (2.0 * math.pi / length)
    return jnp.concatenate([jnp.cos(phase), -jnp.sin(phase)], axis=1).astype(jnp.bfloat16)


def inverse_time_table(length, bins):
    rows = jnp.arange(bins, dtype=jnp.int32)[:, None]
    cols = jnp.arange(length, dtype=jnp.int32)[None, :]
    phase = (rows * cols % length).astype(jnp.float32) * (2.0 * math.pi / length)
    weight = jnp.where(rows == 0, 1.0, 2.0).astype(jnp.float32) / length
    return jnp.stack([weight * jnp.cos(phase), -weight * jnp.sin(phase)]).astype(jnp.bfloat16)


def block_table(order_len, exponent_sign):
    rows = jnp.arange(order_len, dtype=jnp.int32)[:, None]
    cols = jnp.arange(order_len, dtype=jnp.int32)[None, :]
    phase = (rows * cols % order_len).astype(jnp.float32) * (2.0 * math.pi / order_len)
    cosine = jnp.cos(phase)
    sine = exponent_sign * jnp.sin(phase)
    real_row = jnp.stack([cosine, sine], axis=1)
    imag_row = jnp.stack([-sine, cosine], axis=1)
    return jnp.stack([real_row, imag_row], axis=0).astype(jnp.bfloat16)


def twiddle_pair(row_count, col_count, total, exponent_sign):
    rows = jnp.arange(row_count, dtype=jnp.int32)[:, None]
    cols = jnp.arange(col_count, dtype=jnp.int32)[None, :]
    phase = (rows * cols % total).astype(jnp.float32) * (2.0 * math.pi / total)
    return (jnp.cos(phase), exponent_sign * jnp.sin(phase))


def rotate(values, cosine, sine):
    return jnp.stack([values[0] * cosine - values[1] * sine, values[0] * sine + values[1] * cosine])


def bins_body(record, fan_mask):
    channels, span_len = record.shape
    frames_here = span_len // HOP
    taper = hann_taper(WIN)
    forward_time = time_table(WIN, BINS).T
    inverse_time = inverse_time_table(WIN, BINS)
    outer_fwd = block_table(SECTION_A, -1.0)
    inner_fwd = block_table(SECTION_B, -1.0)
    inner_inv = block_table(SECTION_B, 1.0)
    outer_inv = block_table(SECTION_A, 1.0)
    fwd_cos, fwd_sin = twiddle_pair(SECTION_A, SECTION_B, NCH, -1.0)
    inv_cos, inv_sin = twiddle_pair(SECTION_A, SECTION_B, NCH, 1.0)
    fwd_cos = fwd_cos[:, None, None, :]
    fwd_sin = fwd_sin[:, None, None, :]
    inv_cos = inv_cos[:, None, None, :]
    inv_sin = inv_sin[:, None, None, :]
    local_bins = fan_mask.shape[0]
    fk_gate = (
        fan_mask.reshape(local_bins, SECTION_B, SECTION_A).transpose(2, 0, 1).astype(jnp.float32)
    )
    fk_gate = fk_gate[:, :, None, None, :]
    time_major = record.T
    rim_rows = passed_along(time_major[:HOP], "tm", -1)
    extended = jnp.concatenate([time_major, rim_rows], axis=0)
    blocks = extended.reshape(frames_here + 1, HOP, channels).astype(jnp.float32)
    first_half = (blocks[:-1] * taper[:HOP, None]).astype(jnp.bfloat16)
    second_half = (blocks[1:] * taper[HOP:, None]).astype(jnp.bfloat16)
    spectra = jnp.einsum(
        "jn,fnc->jfc", forward_time[:, :HOP], first_half, preferred_element_type=jnp.float32
    )
    spectra = spectra + jnp.einsum(
        "jn,fnc->jfc", forward_time[:, HOP:], second_half, preferred_element_type=jnp.float32
    )
    spectra = spectra.astype(jnp.bfloat16).reshape(2, BINS, frames_here, channels)
    bin_grid = lax.all_to_all(spectra, "chan", split_axis=1, concat_axis=3, tiled=True)
    bin_count = bin_grid.shape[1]
    item_count = bin_grid.shape[2]
    split_grid = bin_grid.reshape(2, bin_count, item_count, SECTION_A, SECTION_B)
    section_one = jnp.einsum(
        "ipoj,ikfpq->ojkfq", outer_fwd, split_grid, preferred_element_type=jnp.float32
    )
    section_one = rotate(section_one, fwd_cos, fwd_sin).astype(jnp.bfloat16)
    fk_plane = jnp.einsum(
        "ijkfq,iqor->jkfor", section_one, inner_fwd, preferred_element_type=jnp.float32
    )
    fk_plane = (fk_plane * fk_gate).astype(jnp.bfloat16)
    section_three = jnp.einsum(
        "jkfir,iroq->jkfoq", fk_plane, inner_inv, preferred_element_type=jnp.float32
    )
    real_part = section_three[:, :, :, 0]
    imag_part = section_three[:, :, :, 1]
    section_three = jnp.stack(
        [real_part * inv_cos - imag_part * inv_sin, real_part * inv_sin + imag_part * inv_cos]
    ).astype(jnp.bfloat16)
    restored = jnp.einsum(
        "ijkfq,ijop->opkfq", section_three, outer_inv, preferred_element_type=jnp.float32
    )
    restored = (restored * (1.0 / NCH)).astype(jnp.bfloat16)
    restored = restored.transpose(0, 2, 3, 1, 4).reshape(2, bin_count, item_count, NCH)
    returned = lax.all_to_all(restored, "chan", split_axis=3, concat_axis=1, tiled=True)
    signal = jnp.einsum("ikn,ikfc->nfc", inverse_time, returned, preferred_element_type=jnp.float32)
    head_half = signal[:HOP]
    tail_half = signal[HOP:]
    carried = passed_along(tail_half[:, -1].astype(jnp.bfloat16), "tm", 1).astype(jnp.float32)
    output_blocks = head_half + jnp.concatenate([carried[:, None], tail_half[:, :-1]], axis=1)
    return output_blocks.transpose(2, 1, 0).reshape(channels, span_len)


LANES = 128
GROUP = 8
PITCH_Q = SECTION_A + 1
PITCH_J = SECTION_B + 1


def flat_table(order_len, exponent_sign):
    table = block_table(order_len, exponent_sign)
    return table.transpose(2, 3, 0, 1).reshape(2 * order_len, 2 * order_len)


def frame_kernel(
    first, second, taper, fwd_time, inv_time, w_one, w_two, w_three, w_four,
    tw_cos, tw_sin, gate, head, tail, by_q, by_j, restored,
):
    def rows_at(index, size):
        return pl.ds(pl.multiple_of(index * size, size), size)

    def padded(step, g, size):
        return pl.ds(pl.multiple_of(step * (GROUP * (size + 1)), 8) + g * (size + 1), size)

    parts = fwd_time.shape[0]
    for part in range(parts):
        lanes = slice(part * LANES, (part + 1) * LANES)

        @pl.loop(0, SECTION_A // GROUP)
        def _(step):
            rows = rows_at(step, GROUP * SECTION_B)
            left = (first[rows, :].astype(jnp.float32) * taper[:, :HOP]).astype(jnp.bfloat16)
            right = (second[rows, :].astype(jnp.float32) * taper[:, HOP:]).astype(jnp.bfloat16)
            spectra = jnp.dot(left, fwd_time[part, :HOP], preferred_element_type=jnp.float32)
            spectra += jnp.dot(right, fwd_time[part, HOP:], preferred_element_type=jnp.float32)
            for g in range(GROUP):
                for i in range(2):
                    by_q[i, pl.ds(step * GROUP + g, SECTION_B, stride=PITCH_Q), :] = spectra[
                        g * SECTION_B : (g + 1) * SECTION_B, i * LANES : (i + 1) * LANES
                    ]

        @pl.loop(0, SECTION_B // GROUP)
        def _(step):
            columns = []
            for g in range(GROUP):
                rows = padded(step, g, SECTION_A)
                columns.append(
                    jnp.concatenate([by_q[0, rows, :], by_q[1, rows, :]], axis=0).astype(jnp.bfloat16)
                )
            total = jnp.dot(
                w_one[...], jnp.concatenate(columns, axis=1), preferred_element_type=jnp.float32
            )
            for g in range(GROUP):
                rows = rows_at(step * GROUP + g, SECTION_A)
                cosine, sine = tw_cos[rows, :], tw_sin[rows, :]
                real = total[:SECTION_A, g * LANES : (g + 1) * LANES]
                imag = total[SECTION_A:, g * LANES : (g + 1) * LANES]
                spread = pl.ds(step * GROUP + g, SECTION_A, stride=PITCH_J)
                by_j[0, spread, :] = real * cosine + imag * sine
                by_j[1, spread, :] = imag * cosine - real * sine

        @pl.loop(0, SECTION_A // GROUP)
        def _(step):
            columns, gates = [], []
            for g in range(GROUP):
                rows = rows_at(step * GROUP + g, SECTION_B)
                held = padded(step, g, SECTION_B)
                columns.append(
                    jnp.concatenate([by_j[0, held, :], by_j[1, held, :]], axis=0).astype(jnp.bfloat16)
                )
                gates.append(gate[rows, lanes].astype(jnp.float32))
            plane = jnp.dot(
                w_two[...], jnp.concatenate(columns, axis=1), preferred_element_type=jnp.float32
            )
            passing = jnp.concatenate(gates, axis=1)
            plane = plane * jnp.concatenate([passing, passing], axis=0)
            total = jnp.dot(
                w_three[...], plane.astype(jnp.bfloat16), preferred_element_type=jnp.float32
            )
            for g in range(GROUP):
                spread = pl.ds(step * GROUP + g, SECTION_B, stride=PITCH_Q)
                for i in range(2):
                    by_q[i, spread, :] = total[
                        i * SECTION_B : (i + 1) * SECTION_B, g * LANES : (g + 1) * LANES
                    ]

        @pl.loop(0, SECTION_B // GROUP)
        def _(step):
            columns = []
            for g in range(GROUP):
                rows = rows_at(step * GROUP + g, SECTION_A)
                cosine, sine = tw_cos[rows, :], tw_sin[rows, :]
                held = padded(step, g, SECTION_A)
                real, imag = by_q[0, held, :], by_q[1, held, :]
                columns.append(
                    jnp.concatenate(
                        [real * cosine - imag * sine, real * sine + imag * cosine], axis=0
                    ).astype(jnp.bfloat16)
                )
            total = jnp.dot(
                w_four[...], jnp.concatenate(columns, axis=1), preferred_element_type=jnp.float32
            ) * (1.0 / NCH)
            for g in range(GROUP):
                spread = pl.ds(step * GROUP + g, SECTION_A, stride=PITCH_J)
                for i in range(2):
                    by_j[i, spread, :] = total[
                        i * SECTION_A : (i + 1) * SECTION_A, g * LANES : (g + 1) * LANES
                    ]

        @pl.loop(0, SECTION_A // GROUP)
        def _(step):
            for i in range(2):
                at = (2 * part + i) * LANES
                for g in range(GROUP):
                    rows = rows_at(step * GROUP + g, SECTION_B)
                    restored[rows, at : at + LANES] = by_j[i, padded(step, g, SECTION_B), :].astype(
                        jnp.bfloat16
                    )

    @pl.loop(0, SECTION_A // GROUP)
    def _(step):
        rows = rows_at(step, GROUP * SECTION_B)
        signal = jnp.dot(restored[rows, :], inv_time[...], preferred_element_type=jnp.float32)
        head[rows, :] = signal[:, :HOP].astype(head.dtype)
        tail[rows, :] = signal[:, HOP:].astype(tail.dtype)


def frame_tables():
    parts = BINS // LANES
    fwd_time = time_table(WIN, BINS).reshape(WIN, 2, parts, LANES)
    fwd_time = fwd_time.transpose(2, 0, 1, 3).reshape(parts, WIN, 2 * LANES)
    inv_time = inverse_time_table(WIN, BINS).reshape(2, parts, LANES, WIN)
    inv_time = inv_time.transpose(1, 0, 2, 3).reshape(2 * BINS, WIN)
    tw_cos, tw_sin = twiddle_pair(SECTION_B, SECTION_A, NCH, 1.0)
    spread = (SECTION_B, SECTION_A, LANES)
    return (
        hann_taper(WIN)[None, :],
        fwd_time,
        inv_time,
        flat_table(SECTION_A, -1.0),
        flat_table(SECTION_B, -1.0),
        flat_table(SECTION_B, 1.0),
        flat_table(SECTION_A, 1.0),
        jnp.broadcast_to(tw_cos[:, :, None], spread).reshape(NCH, LANES),
        jnp.broadcast_to(tw_sin[:, :, None], spread).reshape(NCH, LANES),
    )


def filter_frame(first, second, tables, gate):
    half = jax.ShapeDtypeStruct((NCH, HOP), jnp.bfloat16)
    whole = pl.BlockSpec(memory_space=pltpu.VMEM)
    return pl.pallas_call(
        frame_kernel,
        out_shape=(half, half),
        in_specs=[whole] * (3 + len(tables)),
        out_specs=(whole, whole),
        scratch_shapes=[
            pltpu.VMEM((2, SECTION_B * PITCH_Q, LANES), jnp.float32),
            pltpu.VMEM((2, SECTION_A * PITCH_J, LANES), jnp.float32),
            pltpu.VMEM((NCH, 2 * BINS), jnp.bfloat16),
        ],
        compiler_params=pltpu.CompilerParams(vmem_limit_bytes=60 * 1024 * 1024),
        cost_estimate=pl.CostEstimate(
            flops=16_000_000_000, bytes_accessed=30_000_000, transcendentals=0
        ),
    )(first, second, *tables, gate)


def shifted(value, by):
    axes = ("tm", "chan")
    peers = lax.axis_size("tm") * lax.axis_size("chan")
    pairs = [(i, i + by) for i in range(peers) if 0 <= i + by < peers]
    return lax.ppermute(value, axes, pairs)


def frames_body(record, fan_mask):
    channels, span_len = record.shape
    local_bins = fan_mask.shape[0]
    gate = fan_mask.astype(jnp.bfloat16).reshape(local_bins, SECTION_B, SECTION_A)
    gate = gate.transpose(0, 2, 1).reshape(local_bins, NCH)
    gate = lax.all_gather(gate, "chan", axis=0, tiled=True).T
    tables = frame_tables()
    mine = lax.all_to_all(record, "chan", split_axis=1, concat_axis=0, tiled=True)
    after = shifted(mine[:, :HOP], -1)
    held = mine.shape[1] // HOP
    blocks = [mine[:, f * HOP : (f + 1) * HOP] for f in range(held)] + [after]
    halves = [filter_frame(blocks[f], blocks[f + 1], tables, gate) for f in range(held)]
    before = shifted(halves[-1][1], 1)
    tails = [before] + [halves[f][1] for f in range(held - 1)]
    sums = [
        (halves[f][0].astype(jnp.float32) + tails[f].astype(jnp.float32)).astype(jnp.bfloat16)
        for f in range(held)
    ]
    result = sums[0] if held == 1 else jnp.concatenate(sums, axis=1)
    result = lax.all_to_all(result, "chan", split_axis=0, concat_axis=1, tiled=True)
    return result.astype(jnp.float32)


def body(record, fan_mask):
    if (record.shape[1] // HOP) % lax.axis_size("chan") == 0:
        return frames_body(record, fan_mask)
    return bins_body(record, fan_mask)


def solution(mesh):
    placed = (P("chan", "tm"), P("chan", None))
    return jax.shard_map(
        body, mesh=mesh, in_specs=placed, out_specs=P("chan", "tm"), check_vma=False
    )
```

```python
import functools
import math

import jax
import jax.numpy as jnp
from jax import lax
from jax.experimental import pallas as pl
from jax.experimental.pallas import tpu as pltpu
from jax.sharding import PartitionSpec as P

NCH = 8192
SECTION_A = 64
WIN = 512
SECTION_B = 128
HOP = 256
BINS = 256


def passed_along(value, axis, by):
    peers = lax.axis_size(axis)
    pairs = [(i, i + by) for i in range(peers) if 0 <= i + by < peers]
    return lax.ppermute(value, axis, pairs)


def hann_taper(length):
    steps = jnp.arange(length, dtype=jnp.int32).astype(jnp.float32)
    return 0.5 - 0.5 * jnp.cos(steps * (2.0 * math.pi / length))


def time_table(length, bins):
    rows = jnp.arange(length, dtype=jnp.int32)[:, None]
    cols = jnp.arange(bins, dtype=jnp.int32)[None, :]
    phase = (rows * cols % length).astype(jnp.float32) * (2.0 * math.pi / length)
    return jnp.concatenate([jnp.cos(phase), -jnp.sin(phase)], axis=1).astype(jnp.bfloat16)


def inverse_time_table(length, bins):
    rows = jnp.arange(bins, dtype=jnp.int32)[:, None]
    cols = jnp.arange(length, dtype=jnp.int32)[None, :]
    phase = (rows * cols % length).astype(jnp.float32) * (2.0 * math.pi / length)
    weight = jnp.where(rows == 0, 1.0, 2.0).astype(jnp.float32) / length
    return jnp.stack([weight * jnp.cos(phase), -weight * jnp.sin(phase)]).astype(jnp.bfloat16)


def block_table(order_len, exponent_sign):
    rows = jnp.arange(order_len, dtype=jnp.int32)[:, None]
    cols = jnp.arange(order_len, dtype=jnp.int32)[None, :]
    phase = (rows * cols % order_len).astype(jnp.float32) * (2.0 * math.pi / order_len)
    cosine = jnp.cos(phase)
    sine = exponent_sign * jnp.sin(phase)
    real_row = jnp.stack([cosine, sine], axis=1)
    imag_row = jnp.stack([-sine, cosine], axis=1)
    return jnp.stack([real_row, imag_row], axis=0).astype(jnp.bfloat16)


def twiddle_pair(row_count, col_count, total, exponent_sign):
    rows = jnp.arange(row_count, dtype=jnp.int32)[:, None]
    cols = jnp.arange(col_count, dtype=jnp.int32)[None, :]
    phase = (rows * cols % total).astype(jnp.float32) * (2.0 * math.pi / total)
    return (jnp.cos(phase), exponent_sign * jnp.sin(phase))


def rotate(values, cosine, sine):
    return jnp.stack([values[0] * cosine - values[1] * sine, values[0] * sine + values[1] * cosine])


def bins_body(record, fan_mask):
    channels, span_len = record.shape
    frames_here = span_len // HOP
    taper = hann_taper(WIN)
    forward_time = time_table(WIN, BINS).T
    inverse_time = inverse_time_table(WIN, BINS)
    outer_fwd = block_table(SECTION_A, -1.0)
    inner_fwd = block_table(SECTION_B, -1.0)
    inner_inv = block_table(SECTION_B, 1.0)
    outer_inv = block_table(SECTION_A, 1.0)
    fwd_cos, fwd_sin = twiddle_pair(SECTION_A, SECTION_B, NCH, -1.0)
    inv_cos, inv_sin = twiddle_pair(SECTION_A, SECTION_B, NCH, 1.0)
    fwd_cos = fwd_cos[:, None, None, :]
    fwd_sin = fwd_sin[:, None, None, :]
    inv_cos = inv_cos[:, None, None, :]
    inv_sin = inv_sin[:, None, None, :]
    local_bins = fan_mask.shape[0]
    fk_gate = (
        fan_mask.reshape(local_bins, SECTION_B, SECTION_A).transpose(2, 0, 1).astype(jnp.float32)
    )
    fk_gate = fk_gate[:, :, None, None, :]
    time_major = record.T
    rim_rows = passed_along(time_major[:HOP], "tm", -1)
    extended = jnp.concatenate([time_major, rim_rows], axis=0)
    blocks = extended.reshape(frames_here + 1, HOP, channels).astype(jnp.float32)
    first_half = (blocks[:-1] * taper[:HOP, None]).astype(jnp.bfloat16)
    second_half = (blocks[1:] * taper[HOP:, None]).astype(jnp.bfloat16)
    spectra = jnp.einsum(
        "jn,fnc->jfc", forward_time[:, :HOP], first_half, preferred_element_type=jnp.float32
    )
    spectra = spectra + jnp.einsum(
        "jn,fnc->jfc", forward_time[:, HOP:], second_half, preferred_element_type=jnp.float32
    )
    spectra = spectra.astype(jnp.bfloat16).reshape(2, BINS, frames_here, channels)
    bin_grid = lax.all_to_all(spectra, "chan", split_axis=1, concat_axis=3, tiled=True)
    bin_count = bin_grid.shape[1]
    item_count = bin_grid.shape[2]
    split_grid = bin_grid.reshape(2, bin_count, item_count, SECTION_A, SECTION_B)
    section_one = jnp.einsum(
        "ipoj,ikfpq->ojkfq", outer_fwd, split_grid, preferred_element_type=jnp.float32
    )
    section_one = rotate(section_one, fwd_cos, fwd_sin).astype(jnp.bfloat16)
    fk_plane = jnp.einsum(
        "ijkfq,iqor->jkfor", section_one, inner_fwd, preferred_element_type=jnp.float32
    )
    fk_plane = (fk_plane * fk_gate).astype(jnp.bfloat16)
    section_three = jnp.einsum(
        "jkfir,iroq->jkfoq", fk_plane, inner_inv, preferred_element_type=jnp.float32
    )
    real_part = section_three[:, :, :, 0]
    imag_part = section_three[:, :, :, 1]
    section_three = jnp.stack(
        [real_part * inv_cos - imag_part * inv_sin, real_part * inv_sin + imag_part * inv_cos]
    ).astype(jnp.bfloat16)
    restored = jnp.einsum(
        "ijkfq,ijop->opkfq", section_three, outer_inv, preferred_element_type=jnp.float32
    )
    restored = (restored * (1.0 / NCH)).astype(jnp.bfloat16)
    restored = restored.transpose(0, 2, 3, 1, 4).reshape(2, bin_count, item_count, NCH)
    returned = lax.all_to_all(restored, "chan", split_axis=3, concat_axis=1, tiled=True)
    signal = jnp.einsum("ikn,ikfc->nfc", inverse_time, returned, preferred_element_type=jnp.float32)
    head_half = signal[:HOP]
    tail_half = signal[HOP:]
    carried = passed_along(tail_half[:, -1].astype(jnp.bfloat16), "tm", 1).astype(jnp.float32)
    output_blocks = head_half + jnp.concatenate([carried[:, None], tail_half[:, :-1]], axis=1)
    return output_blocks.transpose(2, 1, 0).reshape(channels, span_len)


LANES = 128
GROUP = 8
PITCH_Q = SECTION_A + 1
PITCH_J = SECTION_B + 1


def flat_table(order_len, exponent_sign):
    table = block_table(order_len, exponent_sign)
    return table.transpose(2, 3, 0, 1).reshape(2 * order_len, 2 * order_len)


def frame_kernel(
    first, second, taper, fwd_time, inv_time, w_one, w_two, w_three, w_four,
    tw_cos, tw_sin, gate, head, tail, by_q, by_j, restored,
):
    def rows_at(index, size):
        return pl.ds(pl.multiple_of(index * size, size), size)

    def padded(step, g, size):
        return pl.ds(pl.multiple_of(step * (GROUP * (size + 1)), 8) + g * (size + 1), size)

    parts = fwd_time.shape[0]
    for part in range(parts):
        lanes = slice(part * LANES, (part + 1) * LANES)

        @pl.loop(0, SECTION_A // GROUP)
        def _(step):
            rows = rows_at(step, GROUP * SECTION_B)
            left = (first[rows, :].astype(jnp.float32) * taper[:, :HOP]).astype(jnp.bfloat16)
            right = (second[rows, :].astype(jnp.float32) * taper[:, HOP:]).astype(jnp.bfloat16)
            spectra = jnp.dot(left, fwd_time[part, :HOP], preferred_element_type=jnp.float32)
            spectra += jnp.dot(right, fwd_time[part, HOP:], preferred_element_type=jnp.float32)
            for g in range(GROUP):
                for i in range(2):
                    by_q[i, pl.ds(step * GROUP + g, SECTION_B, stride=PITCH_Q), :] = spectra[
                        g * SECTION_B : (g + 1) * SECTION_B, i * LANES : (i + 1) * LANES
                    ]

        @pl.loop(0, SECTION_B // GROUP)
        def _(step):
            columns = []
            for g in range(GROUP):
                rows = padded(step, g, SECTION_A)
                columns.append(
                    jnp.concatenate([by_q[0, rows, :], by_q[1, rows, :]], axis=0).astype(jnp.bfloat16)
                )
            total = jnp.dot(
                w_one[...], jnp.concatenate(columns, axis=1), preferred_element_type=jnp.float32
            )
            for g in range(GROUP):
                rows = rows_at(step * GROUP + g, SECTION_A)
                cosine, sine = tw_cos[rows, :], tw_sin[rows, :]
                real = total[:SECTION_A, g * LANES : (g + 1) * LANES]
                imag = total[SECTION_A:, g * LANES : (g + 1) * LANES]
                spread = pl.ds(step * GROUP + g, SECTION_A, stride=PITCH_J)
                by_j[0, spread, :] = real * cosine + imag * sine
                by_j[1, spread, :] = imag * cosine - real * sine

        @pl.loop(0, SECTION_A // GROUP)
        def _(step):
            columns, gates = [], []
            for g in range(GROUP):
                rows = rows_at(step * GROUP + g, SECTION_B)
                held = padded(step, g, SECTION_B)
                columns.append(
                    jnp.concatenate([by_j[0, held, :], by_j[1, held, :]], axis=0).astype(jnp.bfloat16)
                )
                gates.append(gate[rows, lanes].astype(jnp.float32))
            plane = jnp.dot(
                w_two[...], jnp.concatenate(columns, axis=1), preferred_element_type=jnp.float32
            )
            passing = jnp.concatenate(gates, axis=1)
            plane = plane * jnp.concatenate([passing, passing], axis=0)
            total = jnp.dot(
                w_three[...], plane.astype(jnp.bfloat16), preferred_element_type=jnp.float32
            )
            for g in range(GROUP):
                spread = pl.ds(step * GROUP + g, SECTION_B, stride=PITCH_Q)
                for i in range(2):
                    by_q[i, spread, :] = total[
                        i * SECTION_B : (i + 1) * SECTION_B, g * LANES : (g + 1) * LANES
                    ]

        @pl.loop(0, SECTION_B // GROUP)
        def _(step):
            columns = []
            for g in range(GROUP):
                rows = rows_at(step * GROUP + g, SECTION_A)
                cosine, sine = tw_cos[rows, :], tw_sin[rows, :]
                held = padded(step, g, SECTION_A)
                real, imag = by_q[0, held, :], by_q[1, held, :]
                columns.append(
                    jnp.concatenate(
                        [real * cosine - imag * sine, real * sine + imag * cosine], axis=0
                    ).astype(jnp.bfloat16)
                )
            total = jnp.dot(
                w_four[...], jnp.concatenate(columns, axis=1), preferred_element_type=jnp.float32
            ) * (1.0 / NCH)
            for g in range(GROUP):
                spread = pl.ds(step * GROUP + g, SECTION_A, stride=PITCH_J)
                for i in range(2):
                    by_j[i, spread, :] = total[
                        i * SECTION_A : (i + 1) * SECTION_A, g * LANES : (g + 1) * LANES
                    ]

        @pl.loop(0, SECTION_A // GROUP)
        def _(step):
            for i in range(2):
                at = (2 * part + i) * LANES
                for g in range(GROUP):
                    rows = rows_at(step * GROUP + g, SECTION_B)
                    restored[rows, at : at + LANES] = by_j[i, padded(step, g, SECTION_B), :].astype(
                        jnp.bfloat16
                    )

    @pl.loop(0, SECTION_A // GROUP)
    def _(step):
        rows = rows_at(step, GROUP * SECTION_B)
        signal = jnp.dot(restored[rows, :], inv_time[...], preferred_element_type=jnp.float32)
        head[rows, :] = signal[:, :HOP].astype(head.dtype)
        tail[rows, :] = signal[:, HOP:].astype(tail.dtype)


def frame_tables():
    parts = BINS // LANES
    fwd_time = time_table(WIN, BINS).reshape(WIN, 2, parts, LANES)
    fwd_time = fwd_time.transpose(2, 0, 1, 3).reshape(parts, WIN, 2 * LANES)
    inv_time = inverse_time_table(WIN, BINS).reshape(2, parts, LANES, WIN)
    inv_time = inv_time.transpose(1, 0, 2, 3).reshape(2 * BINS, WIN)
    tw_cos, tw_sin = twiddle_pair(SECTION_B, SECTION_A, NCH, 1.0)
    spread = (SECTION_B, SECTION_A, LANES)
    return (
        hann_taper(WIN)[None, :],
        fwd_time,
        inv_time,
        flat_table(SECTION_A, -1.0),
        flat_table(SECTION_B, -1.0),
        flat_table(SECTION_B, 1.0),
        flat_table(SECTION_A, 1.0),
        jnp.broadcast_to(tw_cos[:, :, None], spread).reshape(NCH, LANES),
        jnp.broadcast_to(tw_sin[:, :, None], spread).reshape(NCH, LANES),
    )


def filter_frame(first, second, tables, gate):
    half = jax.ShapeDtypeStruct((NCH, HOP), jnp.bfloat16)
    whole = pl.BlockSpec(memory_space=pltpu.VMEM)
    return pl.pallas_call(
        frame_kernel,
        out_shape=(half, half),
        in_specs=[whole] * (3 + len(tables)),
        out_specs=(whole, whole),
        scratch_shapes=[
            pltpu.VMEM((2, SECTION_B * PITCH_Q, LANES), jnp.float32),
            pltpu.VMEM((2, SECTION_A * PITCH_J, LANES), jnp.float32),
            pltpu.VMEM((NCH, 2 * BINS), jnp.bfloat16),
        ],
        compiler_params=pltpu.CompilerParams(vmem_limit_bytes=60 * 1024 * 1024),
        cost_estimate=pl.CostEstimate(
            flops=16_000_000_000, bytes_accessed=30_000_000, transcendentals=0
        ),
    )(first, second, *tables, gate)


def device_at(group, place):
    peers = lax.axis_size("chan")
    place = place + (group % 2) * (peers - 1 - 2 * place)
    if peers % 4 == 0:
        place = place + (place // 4 % 2) * (2 - 4 * (place // 2 % 2))
    return place


def place_of(group, device):
    peers = lax.axis_size("chan")
    if peers % 4 == 0:
        device = device + (device // 4 % 2) * (2 - 4 * (device // 2 % 2))
    return device + (group % 2) * (peers - 1 - 2 * device)


def along_line(group, place, by):
    peers = lax.axis_size("chan")
    spot = group * peers + place + by
    there = spot // peers
    return {"tm": there, "chan": device_at(there, spot % peers)}


def greet(group, me, place):
    groups, peers = lax.axis_size("tm"), lax.axis_size("chan")
    barrier = pltpu.get_barrier_semaphore()

    def signal(target):
        pl.semaphore_signal(barrier, inc=1, device_id=target, device_id_type=pl.DeviceIdType.MESH)

    @pl.loop(1, peers)
    def _(i):
        signal({"tm": group, "chan": lax.rem(me + i, peers)})

    up = jnp.logical_and(place == 0, group > 0)
    down = jnp.logical_and(place == peers - 1, group < groups - 1)

    @pl.when(up)
    def _():
        signal(along_line(group, place, -1))

    @pl.when(down)
    def _():
        signal(along_line(group, place, 1))

    pl.semaphore_wait(barrier, peers - 1 + up.astype(jnp.int32) + down.astype(jnp.int32))


def remote(source, target, send_sem, recv_sem, device):
    return pltpu.make_async_remote_copy(
        src_ref=source,
        dst_ref=target,
        send_sem=send_sem,
        recv_sem=recv_sem,
        device_id=device,
        device_id_type=pl.DeviceIdType.MESH,
    )


def gather_kernel(record, first, second, nothing, send, recv, pass_send, pass_recv, local):
    groups, peers = lax.axis_size("tm"), lax.axis_size("chan")
    group, me = lax.axis_index("tm"), lax.axis_index("chan")
    place = place_of(group, me)
    size = record.shape[0]
    has_prev = jnp.logical_or(place > 0, group > 0)
    has_next = jnp.logical_or(place < peers - 1, group < groups - 1)

    def rows(device):
        return pl.ds(pl.multiple_of(device * size, size), size)

    def block(device):
        return record.at[:, pl.ds(pl.multiple_of(place_of(group, device) * HOP, HOP), HOP)]

    def sent(device):
        return remote(
            block(device), first.at[rows(me)], send.at[device], recv.at[me],
            {"tm": group, "chan": device},
        )

    def arriving(device):
        return remote(
            block(device), first.at[rows(device)], send.at[device], recv.at[device],
            {"tm": group, "chan": device},
        )

    def passed(source, device):
        return remote(
            source, second.at[rows(device)], pass_send.at[device], pass_recv.at[device],
            along_line(group, place, -1),
        )

    greet(group, me, place)
    own = pltpu.make_async_copy(block(me), first.at[rows(me)], local)
    own.start()

    @pl.loop(1, peers)
    def _(i):
        sent(lax.rem(me + i, peers)).start()

    @pl.when(has_prev)
    def _():
        passed(block(me), me).start()

    @pl.loop(1, peers)
    def _(i):
        device = lax.rem(me + peers - i, peers)
        arriving(device).wait_recv()

        @pl.when(has_prev)
        def _():
            passed(first.at[rows(device)], device).start()

    own.wait()

    @pl.loop(1, peers)
    def _(i):
        sent(lax.rem(me + i, peers)).wait_send()

    @pl.when(has_prev)
    def _():
        @pl.loop(0, peers)
        def _(i):
            passed(first.at[rows(i)], i).wait_send()

    @pl.when(has_next)
    def _():
        @pl.loop(0, peers)
        def _(i):
            passed(first.at[rows(i)], i).wait_recv()

    @pl.when(jnp.logical_not(has_next))
    def _():
        nothing[...] = jnp.zeros_like(nothing)

        @pl.loop(0, peers)
        def _(i):
            fill = pltpu.make_async_copy(nothing, second.at[rows(i)], local)
            fill.start()
            fill.wait()


def scatter_kernel(head, tail, out, carried, total, send, recv, pass_send, pass_recv, local):
    groups, peers = lax.axis_size("tm"), lax.axis_size("chan")
    group, me = lax.axis_index("tm"), lax.axis_index("chan")
    place = place_of(group, me)
    size = out.shape[0]
    has_prev = jnp.logical_or(place > 0, group > 0)
    has_next = jnp.logical_or(place < peers - 1, group < groups - 1)
    after = along_line(group, place, 1)

    def rows(device):
        return pl.ds(pl.multiple_of(device * size, size), size)

    def block(device):
        return out.at[:, pl.ds(pl.multiple_of(place_of(group, device) * HOP, HOP), HOP)]

    def passed(device):
        return remote(
            tail.at[rows(device)], carried.at[rows(device)], pass_send.at[device],
            pass_recv.at[device], after,
        )

    def sent(device):
        return remote(
            total.at[rows(device)], block(me), send.at[device], recv.at[me],
            {"tm": group, "chan": device},
        )

    def arriving(device):
        return remote(
            total.at[rows(device)], block(device), send.at[device], recv.at[device],
            {"tm": group, "chan": device},
        )

    def add(device):
        @pl.when(has_prev)
        def _():
            passed(device).wait_recv()
            total[rows(device), :] = (
                head[rows(device), :].astype(jnp.float32)
                + carried[rows(device), :].astype(jnp.float32)
            ).astype(total.dtype)

        @pl.when(jnp.logical_not(has_prev))
        def _():
            total[rows(device), :] = head[rows(device), :]

    greet(group, me, place)

    @pl.when(has_next)
    def _():
        @pl.loop(1, peers + 1)
        def _(i):
            passed(lax.rem(after["chan"] + i, peers)).start()

    @pl.loop(1, peers)
    def _(i):
        device = lax.rem(me + i, peers)
        add(device)
        sent(device).start()

    add(me)
    own = pltpu.make_async_copy(total.at[rows(me)], block(me), local)
    own.start()
    own.wait()

    @pl.loop(1, peers)
    def _(i):
        arriving(lax.rem(me + peers - i, peers)).wait_recv()

    @pl.loop(1, peers)
    def _(i):
        sent(lax.rem(me + i, peers)).wait_send()

    @pl.when(has_next)
    def _():
        @pl.loop(0, peers)
        def _(i):
            passed(i).wait_send()


def exchange_scratch():
    peers = lax.axis_size("chan")
    return [pltpu.SemaphoreType.DMA((peers,))] * 4 + [pltpu.SemaphoreType.DMA]


def gather_frames(record):
    anywhere = pl.BlockSpec(memory_space=pl.ANY)
    half = jax.ShapeDtypeStruct((NCH, HOP), record.dtype)
    return pl.pallas_call(
        gather_kernel,
        out_shape=(half, half),
        in_specs=[anywhere],
        out_specs=(anywhere, anywhere),
        scratch_shapes=[pltpu.VMEM((record.shape[0], HOP), record.dtype)] + exchange_scratch(),
        compiler_params=pltpu.CompilerParams(
            collective_id=0, has_side_effects=True, vmem_limit_bytes=60 * 1024 * 1024
        ),
        cost_estimate=pl.CostEstimate(flops=0, bytes_accessed=300_000_000, transcendentals=0),
    )(record)


def scatter_frames(head, tail, channels, span_len):
    anywhere = pl.BlockSpec(memory_space=pl.ANY)
    return pl.pallas_call(
        scatter_kernel,
        out_shape=jax.ShapeDtypeStruct((channels, span_len), head.dtype),
        in_specs=[pl.BlockSpec(memory_space=pltpu.VMEM), anywhere],
        out_specs=anywhere,
        scratch_shapes=[pltpu.VMEM((NCH, HOP), head.dtype)] * 2 + exchange_scratch(),
        compiler_params=pltpu.CompilerParams(
            collective_id=1, has_side_effects=True, vmem_limit_bytes=60 * 1024 * 1024
        ),
        cost_estimate=pl.CostEstimate(flops=0, bytes_accessed=300_000_000, transcendentals=0),
    )(head, tail)


def frames_body(record, fan_mask):
    channels, span_len = record.shape
    local_bins = fan_mask.shape[0]
    gate = fan_mask.astype(jnp.bfloat16).reshape(local_bins, SECTION_B, SECTION_A)
    gate = gate.transpose(0, 2, 1).reshape(local_bins, NCH)
    gate = lax.all_gather(gate, "chan", axis=0, tiled=True).T
    first, second = gather_frames(record)
    head, tail = filter_frame(first, second, frame_tables(), gate)
    return scatter_frames(head, tail, channels, span_len).astype(jnp.float32)


def body(record, fan_mask):
    if record.shape[1] // HOP == lax.axis_size("chan"):
        return frames_body(record, fan_mask)
    return bins_body(record, fan_mask)


def solution(mesh):
    placed = (P("chan", "tm"), P("chan", None))
    return jax.shard_map(
        body, mesh=mesh, in_specs=placed, out_specs=P("chan", "tm"), check_vma=False
    )
```

```python
import math

import jax
import jax.numpy as jnp
import numpy as np
from jax import lax
from jax.experimental import pallas as pl
from jax.experimental.pallas import tpu as pltpu
from jax.sharding import PartitionSpec as P

NCH = 8192
SECTION_A = 64
WIN = 512
SECTION_B = 128
HOP = 256
BINS = 256


def passed_along(value, axis, by):
    peers = lax.axis_size(axis)
    pairs = [(i, i + by) for i in range(peers) if 0 <= i + by < peers]
    return lax.ppermute(value, axis, pairs)


def hann_taper(length):
    steps = np.arange(length, dtype=jnp.int32).astype(jnp.float32)
    return 0.5 - 0.5 * np.cos(steps * (2.0 * math.pi / length))


def time_table(length, bins):
    rows = np.arange(length, dtype=jnp.int32)[:, None]
    cols = np.arange(bins, dtype=jnp.int32)[None, :]
    phase = (rows * cols % length).astype(jnp.float32) * (2.0 * math.pi / length)
    return np.concatenate([np.cos(phase), -np.sin(phase)], axis=1).astype(jnp.bfloat16)


def inverse_time_table(length, bins):
    rows = np.arange(bins, dtype=jnp.int32)[:, None]
    cols = np.arange(length, dtype=jnp.int32)[None, :]
    phase = (rows * cols % length).astype(jnp.float32) * (2.0 * math.pi / length)
    weight = np.where(rows == 0, 1.0, 2.0).astype(jnp.float32) / length
    return np.stack([weight * np.cos(phase), -weight * np.sin(phase)]).astype(jnp.bfloat16)


def block_table(order_len, exponent_sign):
    rows = np.arange(order_len, dtype=jnp.int32)[:, None]
    cols = np.arange(order_len, dtype=jnp.int32)[None, :]
    phase = (rows * cols % order_len).astype(jnp.float32) * (2.0 * math.pi / order_len)
    cosine = np.cos(phase)
    sine = exponent_sign * np.sin(phase)
    real_row = np.stack([cosine, sine], axis=1)
    imag_row = np.stack([-sine, cosine], axis=1)
    return np.stack([real_row, imag_row], axis=0).astype(jnp.bfloat16)


def twiddle_pair(row_count, col_count, total, exponent_sign):
    rows = np.arange(row_count, dtype=jnp.int32)[:, None]
    cols = np.arange(col_count, dtype=jnp.int32)[None, :]
    phase = (rows * cols % total).astype(jnp.float32) * (2.0 * math.pi / total)
    return (np.cos(phase), exponent_sign * np.sin(phase))


def rotate(values, cosine, sine):
    return jnp.stack([values[0] * cosine - values[1] * sine, values[0] * sine + values[1] * cosine])


def bins_body(record, fan_mask):
    channels, span_len = record.shape
    frames_here = span_len // HOP
    taper = hann_taper(WIN)
    forward_time = time_table(WIN, BINS).T
    inverse_time = inverse_time_table(WIN, BINS)
    outer_fwd = block_table(SECTION_A, -1.0)
    inner_fwd = block_table(SECTION_B, -1.0)
    inner_inv = block_table(SECTION_B, 1.0)
    outer_inv = block_table(SECTION_A, 1.0)
    fwd_cos, fwd_sin = twiddle_pair(SECTION_A, SECTION_B, NCH, -1.0)
    inv_cos, inv_sin = twiddle_pair(SECTION_A, SECTION_B, NCH, 1.0)
    fwd_cos = fwd_cos[:, None, None, :]
    fwd_sin = fwd_sin[:, None, None, :]
    inv_cos = inv_cos[:, None, None, :]
    inv_sin = inv_sin[:, None, None, :]
    local_bins = fan_mask.shape[0]
    fk_gate = (
        fan_mask.reshape(local_bins, SECTION_B, SECTION_A).transpose(2, 0, 1).astype(jnp.float32)
    )
    fk_gate = fk_gate[:, :, None, None, :]
    time_major = record.T
    rim_rows = passed_along(time_major[:HOP], "tm", -1)
    extended = jnp.concatenate([time_major, rim_rows], axis=0)
    blocks = extended.reshape(frames_here + 1, HOP, channels).astype(jnp.float32)
    first_half = (blocks[:-1] * taper[:HOP, None]).astype(jnp.bfloat16)
    second_half = (blocks[1:] * taper[HOP:, None]).astype(jnp.bfloat16)
    spectra = jnp.einsum(
        "jn,fnc->jfc", forward_time[:, :HOP], first_half, preferred_element_type=jnp.float32
    )
    spectra = spectra + jnp.einsum(
        "jn,fnc->jfc", forward_time[:, HOP:], second_half, preferred_element_type=jnp.float32
    )
    spectra = spectra.astype(jnp.bfloat16).reshape(2, BINS, frames_here, channels)
    bin_grid = lax.all_to_all(spectra, "chan", split_axis=1, concat_axis=3, tiled=True)
    bin_count = bin_grid.shape[1]
    item_count = bin_grid.shape[2]
    split_grid = bin_grid.reshape(2, bin_count, item_count, SECTION_A, SECTION_B)
    section_one = jnp.einsum(
        "ipoj,ikfpq->ojkfq", outer_fwd, split_grid, preferred_element_type=jnp.float32
    )
    section_one = rotate(section_one, fwd_cos, fwd_sin).astype(jnp.bfloat16)
    fk_plane = jnp.einsum(
        "ijkfq,iqor->jkfor", section_one, inner_fwd, preferred_element_type=jnp.float32
    )
    fk_plane = (fk_plane * fk_gate).astype(jnp.bfloat16)
    section_three = jnp.einsum(
        "jkfir,iroq->jkfoq", fk_plane, inner_inv, preferred_element_type=jnp.float32
    )
    real_part = section_three[:, :, :, 0]
    imag_part = section_three[:, :, :, 1]
    section_three = jnp.stack(
        [real_part * inv_cos - imag_part * inv_sin, real_part * inv_sin + imag_part * inv_cos]
    ).astype(jnp.bfloat16)
    restored = jnp.einsum(
        "ijkfq,ijop->opkfq", section_three, outer_inv, preferred_element_type=jnp.float32
    )
    restored = (restored * (1.0 / NCH)).astype(jnp.bfloat16)
    restored = restored.transpose(0, 2, 3, 1, 4).reshape(2, bin_count, item_count, NCH)
    returned = lax.all_to_all(restored, "chan", split_axis=3, concat_axis=1, tiled=True)
    signal = jnp.einsum("ikn,ikfc->nfc", inverse_time, returned, preferred_element_type=jnp.float32)
    head_half = signal[:HOP]
    tail_half = signal[HOP:]
    carried = passed_along(tail_half[:, -1].astype(jnp.bfloat16), "tm", 1).astype(jnp.float32)
    output_blocks = head_half + jnp.concatenate([carried[:, None], tail_half[:, :-1]], axis=1)
    return output_blocks.transpose(2, 1, 0).reshape(channels, span_len)


LANES = 128
GROUP = 8
PITCH_Q = SECTION_A + 1
PITCH_J = SECTION_B + 1


def flat_table(order_len, exponent_sign):
    table = block_table(order_len, exponent_sign)
    return table.transpose(2, 3, 0, 1).reshape(2 * order_len, 2 * order_len)


def frame_kernel(
    first, second, taper, fwd_time, inv_time, w_one, w_two, w_three, w_four,
    tw_cos, tw_sin, gate, head, tail, by_q, by_j, restored,
):
    def rows_at(index, size):
        return pl.ds(pl.multiple_of(index * size, size), size)

    def padded(step, g, size):
        return pl.ds(pl.multiple_of(step * (GROUP * (size + 1)), 8) + g * (size + 1), size)

    parts = fwd_time.shape[0]
    for part in range(parts):
        lanes = slice(part * LANES, (part + 1) * LANES)

        @pl.loop(0, SECTION_A // GROUP)
        def _(step):
            rows = rows_at(step, GROUP * SECTION_B)
            left = (first[rows, :].astype(jnp.float32) * taper[:, :HOP]).astype(jnp.bfloat16)
            right = (second[rows, :].astype(jnp.float32) * taper[:, HOP:]).astype(jnp.bfloat16)
            spectra = jnp.dot(left, fwd_time[part, :HOP], preferred_element_type=jnp.float32)
            spectra += jnp.dot(right, fwd_time[part, HOP:], preferred_element_type=jnp.float32)
            for g in range(GROUP):
                for i in range(2):
                    by_q[i, pl.ds(step * GROUP + g, SECTION_B, stride=PITCH_Q), :] = spectra[
                        g * SECTION_B : (g + 1) * SECTION_B, i * LANES : (i + 1) * LANES
                    ]

        @pl.loop(0, SECTION_B // GROUP)
        def _(step):
            columns = []
            for g in range(GROUP):
                rows = padded(step, g, SECTION_A)
                columns.append(
                    jnp.concatenate([by_q[0, rows, :], by_q[1, rows, :]], axis=0).astype(jnp.bfloat16)
                )
            total = jnp.dot(
                w_one[...], jnp.concatenate(columns, axis=1), preferred_element_type=jnp.float32
            )
            for g in range(GROUP):
                rows = rows_at(step * GROUP + g, SECTION_A)
                cosine, sine = tw_cos[rows, :], tw_sin[rows, :]
                real = total[:SECTION_A, g * LANES : (g + 1) * LANES]
                imag = total[SECTION_A:, g * LANES : (g + 1) * LANES]
                spread = pl.ds(step * GROUP + g, SECTION_A, stride=PITCH_J)
                by_j[0, spread, :] = real * cosine + imag * sine
                by_j[1, spread, :] = imag * cosine - real * sine

        @pl.loop(0, SECTION_A // GROUP)
        def _(step):
            columns, gates = [], []
            for g in range(GROUP):
                rows = rows_at(step * GROUP + g, SECTION_B)
                held = padded(step, g, SECTION_B)
                columns.append(
                    jnp.concatenate([by_j[0, held, :], by_j[1, held, :]], axis=0).astype(jnp.bfloat16)
                )
                gates.append(gate[lanes, rows].astype(jnp.float32).T)
            plane = jnp.dot(
                w_two[...], jnp.concatenate(columns, axis=1), preferred_element_type=jnp.float32
            )
            passing = jnp.concatenate(gates, axis=1)
            plane = plane * jnp.concatenate([passing, passing], axis=0)
            total = jnp.dot(
                w_three[...], plane.astype(jnp.bfloat16), preferred_element_type=jnp.float32
            )
            for g in range(GROUP):
                spread = pl.ds(step * GROUP + g, SECTION_B, stride=PITCH_Q)
                for i in range(2):
                    by_q[i, spread, :] = total[
                        i * SECTION_B : (i + 1) * SECTION_B, g * LANES : (g + 1) * LANES
                    ]

        @pl.loop(0, SECTION_B // GROUP)
        def _(step):
            columns = []
            for g in range(GROUP):
                rows = rows_at(step * GROUP + g, SECTION_A)
                cosine, sine = tw_cos[rows, :], tw_sin[rows, :]
                held = padded(step, g, SECTION_A)
                real, imag = by_q[0, held, :], by_q[1, held, :]
                columns.append(
                    jnp.concatenate(
                        [real * cosine - imag * sine, real * sine + imag * cosine], axis=0
                    ).astype(jnp.bfloat16)
                )
            total = jnp.dot(
                w_four[...], jnp.concatenate(columns, axis=1), preferred_element_type=jnp.float32
            ) * (1.0 / NCH)
            for g in range(GROUP):
                spread = pl.ds(step * GROUP + g, SECTION_A, stride=PITCH_J)
                for i in range(2):
                    by_j[i, spread, :] = total[
                        i * SECTION_A : (i + 1) * SECTION_A, g * LANES : (g + 1) * LANES
                    ]

        @pl.loop(0, SECTION_A // GROUP)
        def _(step):
            for i in range(2):
                at = (2 * part + i) * LANES
                for g in range(GROUP):
                    rows = rows_at(step * GROUP + g, SECTION_B)
                    restored[rows, at : at + LANES] = by_j[i, padded(step, g, SECTION_B), :].astype(
                        jnp.bfloat16
                    )

    @pl.loop(0, SECTION_A // GROUP)
    def _(step):
        rows = rows_at(step, GROUP * SECTION_B)
        signal = jnp.dot(restored[rows, :], inv_time[...], preferred_element_type=jnp.float32)
        head[rows, :] = signal[:, :HOP].astype(head.dtype)
        tail[rows, :] = signal[:, HOP:].astype(tail.dtype)


def frame_tables():
    parts = BINS // LANES
    fwd_time = time_table(WIN, BINS).reshape(WIN, 2, parts, LANES)
    fwd_time = fwd_time.transpose(2, 0, 1, 3).reshape(parts, WIN, 2 * LANES)
    inv_time = inverse_time_table(WIN, BINS).reshape(2, parts, LANES, WIN)
    inv_time = inv_time.transpose(1, 0, 2, 3).reshape(2 * BINS, WIN)
    tw_cos, tw_sin = twiddle_pair(SECTION_B, SECTION_A, NCH, 1.0)
    spread = (SECTION_B, SECTION_A, LANES)
    return (
        hann_taper(WIN)[None, :],
        fwd_time,
        inv_time,
        flat_table(SECTION_A, -1.0),
        flat_table(SECTION_B, -1.0),
        flat_table(SECTION_B, 1.0),
        flat_table(SECTION_A, 1.0),
        np.broadcast_to(tw_cos[:, :, None], spread).reshape(NCH, LANES),
        np.broadcast_to(tw_sin[:, :, None], spread).reshape(NCH, LANES),
    )


def filter_frame(first, second, tables, gate):
    half = jax.ShapeDtypeStruct((NCH, HOP), jnp.bfloat16)
    whole = pl.BlockSpec(memory_space=pltpu.VMEM)
    return pl.pallas_call(
        frame_kernel,
        out_shape=(half, half),
        in_specs=[whole] * (3 + len(tables)),
        out_specs=(whole, whole),
        scratch_shapes=[
            pltpu.VMEM((2, SECTION_B * PITCH_Q, LANES), jnp.float32),
            pltpu.VMEM((2, SECTION_A * PITCH_J, LANES), jnp.float32),
            pltpu.VMEM((NCH, 2 * BINS), jnp.bfloat16),
        ],
        compiler_params=pltpu.CompilerParams(vmem_limit_bytes=60 * 1024 * 1024),
        cost_estimate=pl.CostEstimate(
            flops=16_000_000_000, bytes_accessed=30_000_000, transcendentals=0
        ),
    )(first, second, *tables, gate)


def device_at(group, place):
    peers = lax.axis_size("chan")
    place = place + (group % 2) * (peers - 1 - 2 * place)
    if peers % 4 == 0:
        place = place + (place // 4 % 2) * (2 - 4 * (place // 2 % 2))
    return place


def place_of(group, device):
    peers = lax.axis_size("chan")
    if peers % 4 == 0:
        device = device + (device // 4 % 2) * (2 - 4 * (device // 2 % 2))
    return device + (group % 2) * (peers - 1 - 2 * device)


def along_line(group, place, by):
    peers = lax.axis_size("chan")
    spot = group * peers + place + by
    there = spot // peers
    return {"tm": there, "chan": device_at(there, spot % peers)}


def offset_of(step):
    peers = lax.axis_size("chan")
    if peers % 2 == 1:
        return step + 1
    return peers // 2 + (1 - 2 * (step % 2)) * ((step + 1) // 2)


def greet(group, me, place):
    groups, peers = lax.axis_size("tm"), lax.axis_size("chan")
    barrier = pltpu.get_barrier_semaphore()

    def signal(target):
        pl.semaphore_signal(barrier, inc=1, device_id=target, device_id_type=pl.DeviceIdType.MESH)

    @pl.loop(1, peers)
    def _(i):
        signal({"tm": group, "chan": lax.rem(me + i, peers)})

    up = jnp.logical_and(place == 0, group > 0)
    down = jnp.logical_and(place == peers - 1, group < groups - 1)

    @pl.when(up)
    def _():
        signal(along_line(group, place, -1))

    @pl.when(down)
    def _():
        signal(along_line(group, place, 1))

    pl.semaphore_wait(barrier, peers - 1 + up.astype(jnp.int32) + down.astype(jnp.int32))


def remote(source, target, send_sem, recv_sem, device):
    return pltpu.make_async_remote_copy(
        src_ref=source,
        dst_ref=target,
        send_sem=send_sem,
        recv_sem=recv_sem,
        device_id=device,
        device_id_type=pl.DeviceIdType.MESH,
    )


EDGE = 4


def edge_places():
    peers = lax.axis_size("chan")
    return list(range(EDGE, peers, EDGE)) if peers % EDGE == 0 else []


def gather_kernel(record, first, second, nothing, send, recv, pass_send, pass_recv, local, edge_send):
    groups, peers = lax.axis_size("tm"), lax.axis_size("chan")
    group, me = lax.axis_index("tm"), lax.axis_index("chan")
    place = place_of(group, me)
    size = record.shape[0]
    has_prev = jnp.logical_or(place > 0, group > 0)
    has_next = jnp.logical_or(place < peers - 1, group < groups - 1)

    edges = edge_places()
    starts = jnp.logical_and(place > 0, place % EDGE == 0) if edges else place < 0
    ends = jnp.logical_and(place < peers - 1, place % EDGE == EDGE - 1) if edges else place < 0
    passes = jnp.logical_and(has_prev, jnp.logical_not(starts))

    def rows(device):
        return pl.ds(pl.multiple_of(device * size, size), size)

    def block_at(spot):
        return record.at[:, pl.ds(pl.multiple_of(spot * HOP, HOP), HOP)]

    def block(device):
        return block_at(place_of(group, device))

    def edged(at, edge, device):
        return remote(
            block_at(edge), second.at[rows(me)], edge_send.at[at], pass_recv.at[me],
            {"tm": group, "chan": device},
        )

    def sent(device):
        return remote(
            block(device), first.at[rows(me)], send.at[device], recv.at[me],
            {"tm": group, "chan": device},
        )

    def arriving(device):
        return remote(
            block(device), first.at[rows(device)], send.at[device], recv.at[device],
            {"tm": group, "chan": device},
        )

    def passed(source, device):
        return remote(
            source, second.at[rows(device)], pass_send.at[device], pass_recv.at[device],
            along_line(group, place, -1),
        )

    greet(group, me, place)
    own = pltpu.make_async_copy(block(me), first.at[rows(me)], local)
    own.start()

    @pl.loop(0, peers - 1)
    def _(i):
        sent(lax.rem(me + offset_of(i), peers)).start()

    for at, edge in enumerate(edges):
        to = device_at(group, edge - 1)

        @pl.when(to != me)
        def _():
            edged(at, edge, to).start()

        @pl.when(to == me)
        def _():
            pltpu.make_async_copy(block_at(edge), second.at[rows(me)], edge_send.at[at]).start()

    @pl.when(passes)
    def _():
        passed(block(me), me).start()

    @pl.loop(0, peers - 1)
    def _(i):
        device = lax.rem(me + peers - offset_of(i), peers)
        arriving(device).wait_recv()

        @pl.when(passes)
        def _():
            passed(first.at[rows(device)], device).start()

    own.wait()

    @pl.loop(1, peers)
    def _(i):
        sent(lax.rem(me + i, peers)).wait_send()

    @pl.when(passes)
    def _():
        @pl.loop(0, peers)
        def _(i):
            passed(first.at[rows(i)], i).wait_send()

    for at, edge in enumerate(edges):
        to = device_at(group, edge - 1)

        @pl.when(to != me)
        def _():
            edged(at, edge, to).wait_send()

        @pl.when(to == me)
        def _():
            pltpu.make_async_copy(block_at(edge), second.at[rows(me)], edge_send.at[at]).wait()

    @pl.when(has_next)
    def _():
        @pl.loop(1, peers)
        def _(i):
            device = lax.rem(me + i, peers)
            passed(first.at[rows(device)], device).wait_recv()

    @pl.when(jnp.logical_and(has_next, jnp.logical_not(ends)))
    def _():
        passed(first.at[rows(me)], me).wait_recv()

    @pl.when(jnp.logical_not(has_next))
    def _():
        nothing[...] = jnp.zeros_like(nothing)

        @pl.loop(0, peers)
        def _(i):
            fill = pltpu.make_async_copy(nothing, second.at[rows(i)], local)
            fill.start()
            fill.wait()


def scatter_kernel(head, tail, out, carried, total, send, recv, pass_send, pass_recv, local):
    groups, peers = lax.axis_size("tm"), lax.axis_size("chan")
    group, me = lax.axis_index("tm"), lax.axis_index("chan")
    place = place_of(group, me)
    size = out.shape[0]
    has_prev = jnp.logical_or(place > 0, group > 0)
    has_next = jnp.logical_or(place < peers - 1, group < groups - 1)
    after = along_line(group, place, 1)

    def rows(device):
        return pl.ds(pl.multiple_of(device * size, size), size)

    def block(device):
        return out.at[:, pl.ds(pl.multiple_of(place_of(group, device) * HOP, HOP), HOP)]

    def passed(device):
        return remote(
            tail.at[rows(device)], carried.at[rows(device)], pass_send.at[device],
            pass_recv.at[device], after,
        )

    def sent(device):
        return remote(
            total.at[rows(device)], block(me), send.at[device], recv.at[me],
            {"tm": group, "chan": device},
        )

    def arriving(device):
        return remote(
            total.at[rows(device)], block(device), send.at[device], recv.at[device],
            {"tm": group, "chan": device},
        )

    def add(device):
        @pl.when(has_prev)
        def _():
            passed(device).wait_recv()
            total[rows(device), :] = (
                head[rows(device), :].astype(jnp.float32)
                + carried[rows(device), :].astype(jnp.float32)
            ).astype(total.dtype)

        @pl.when(jnp.logical_not(has_prev))
        def _():
            total[rows(device), :] = head[rows(device), :]

    greet(group, me, place)

    @pl.when(has_next)
    def _():
        @pl.loop(0, peers - 1)
        def _(i):
            passed(lax.rem(after["chan"] + offset_of(i), peers)).start()

        passed(after["chan"]).start()

    @pl.loop(0, peers - 1)
    def _(i):
        device = lax.rem(me + offset_of(i), peers)
        add(device)
        sent(device).start()

    add(me)
    own = pltpu.make_async_copy(total.at[rows(me)], block(me), local)
    own.start()
    own.wait()

    @pl.loop(1, peers)
    def _(i):
        arriving(lax.rem(me + peers - i, peers)).wait_recv()

    @pl.loop(1, peers)
    def _(i):
        sent(lax.rem(me + i, peers)).wait_send()

    @pl.when(has_next)
    def _():
        @pl.loop(0, peers)
        def _(i):
            passed(i).wait_send()


def exchange_scratch():
    peers = lax.axis_size("chan")
    return [pltpu.SemaphoreType.DMA((peers,))] * 4 + [pltpu.SemaphoreType.DMA]


def gather_frames(record):
    anywhere = pl.BlockSpec(memory_space=pl.ANY)
    half = jax.ShapeDtypeStruct((NCH, HOP), record.dtype)
    return pl.pallas_call(
        gather_kernel,
        out_shape=(half, half),
        in_specs=[anywhere],
        out_specs=(anywhere, anywhere),
        scratch_shapes=[pltpu.VMEM((record.shape[0], HOP), record.dtype)] + exchange_scratch()
        + [pltpu.SemaphoreType.DMA((max(len(edge_places()), 1),))],
        compiler_params=pltpu.CompilerParams(
            collective_id=0, has_side_effects=True, vmem_limit_bytes=60 * 1024 * 1024
        ),
        cost_estimate=pl.CostEstimate(flops=0, bytes_accessed=300_000_000, transcendentals=0),
    )(record)


def scatter_frames(head, tail, channels, span_len):
    anywhere = pl.BlockSpec(memory_space=pl.ANY)
    return pl.pallas_call(
        scatter_kernel,
        out_shape=jax.ShapeDtypeStruct((channels, span_len), head.dtype),
        in_specs=[pl.BlockSpec(memory_space=pltpu.VMEM), anywhere],
        out_specs=anywhere,
        scratch_shapes=[pltpu.VMEM((NCH, HOP), head.dtype)] * 2 + exchange_scratch(),
        compiler_params=pltpu.CompilerParams(
            collective_id=1, has_side_effects=True, vmem_limit_bytes=60 * 1024 * 1024
        ),
        cost_estimate=pl.CostEstimate(flops=0, bytes_accessed=300_000_000, transcendentals=0),
    )(head, tail)


def frames_body(record, fan_mask):
    channels, span_len = record.shape
    local_bins = fan_mask.shape[0]
    gate = fan_mask.astype(jnp.bfloat16).reshape(local_bins, SECTION_B, SECTION_A)
    gate = gate.transpose(0, 2, 1).reshape(local_bins, NCH)
    gate = lax.all_gather(gate, "chan", axis=0, tiled=True)
    first, second = gather_frames(record)
    head, tail = filter_frame(first, second, frame_tables(), gate)
    return scatter_frames(head, tail, channels, span_len).astype(jnp.float32)


def body(record, fan_mask):
    if record.shape[1] // HOP == lax.axis_size("chan"):
        return frames_body(record, fan_mask)
    return bins_body(record, fan_mask)


def solution(mesh):
    placed = (P("chan", "tm"), P("chan", None))
    return jax.shard_map(
        body, mesh=mesh, in_specs=placed, out_specs=P("chan", "tm"), check_vma=False
    )
```

```python
import math

import jax
import jax.numpy as jnp
import numpy as np
from jax import lax
from jax.experimental import pallas as pl
from jax.experimental.pallas import tpu as pltpu
from jax.sharding import PartitionSpec as P

NCH = 8192
SECTION_A = 64
WIN = 512
SECTION_B = 128
HOP = 256
BINS = 256


def passed_along(value, axis, by):
    peers = lax.axis_size(axis)
    pairs = [(i, i + by) for i in range(peers) if 0 <= i + by < peers]
    return lax.ppermute(value, axis, pairs)


def hann_taper(length):
    steps = np.arange(length, dtype=jnp.int32).astype(jnp.float32)
    return 0.5 - 0.5 * np.cos(steps * (2.0 * math.pi / length))


def time_table(length, bins):
    rows = np.arange(length, dtype=jnp.int32)[:, None]
    cols = np.arange(bins, dtype=jnp.int32)[None, :]
    phase = (rows * cols % length).astype(jnp.float32) * (2.0 * math.pi / length)
    return np.concatenate([np.cos(phase), -np.sin(phase)], axis=1).astype(jnp.bfloat16)


def inverse_time_table(length, bins):
    rows = np.arange(bins, dtype=jnp.int32)[:, None]
    cols = np.arange(length, dtype=jnp.int32)[None, :]
    phase = (rows * cols % length).astype(jnp.float32) * (2.0 * math.pi / length)
    weight = np.where(rows == 0, 1.0, 2.0).astype(jnp.float32) / length
    return np.stack([weight * np.cos(phase), -weight * np.sin(phase)]).astype(jnp.bfloat16)


def block_table(order_len, exponent_sign):
    rows = np.arange(order_len, dtype=jnp.int32)[:, None]
    cols = np.arange(order_len, dtype=jnp.int32)[None, :]
    phase = (rows * cols % order_len).astype(jnp.float32) * (2.0 * math.pi / order_len)
    cosine = np.cos(phase)
    sine = exponent_sign * np.sin(phase)
    real_row = np.stack([cosine, sine], axis=1)
    imag_row = np.stack([-sine, cosine], axis=1)
    return np.stack([real_row, imag_row], axis=0).astype(jnp.bfloat16)


def twiddle_pair(row_count, col_count, total, exponent_sign):
    rows = np.arange(row_count, dtype=jnp.int32)[:, None]
    cols = np.arange(col_count, dtype=jnp.int32)[None, :]
    phase = (rows * cols % total).astype(jnp.float32) * (2.0 * math.pi / total)
    return (np.cos(phase), exponent_sign * np.sin(phase))


def rotate(values, cosine, sine):
    return jnp.stack([values[0] * cosine - values[1] * sine, values[0] * sine + values[1] * cosine])


def bins_body(record, fan_mask):
    channels, span_len = record.shape
    frames_here = span_len // HOP
    taper = hann_taper(WIN)
    forward_time = time_table(WIN, BINS).T
    inverse_time = inverse_time_table(WIN, BINS)
    outer_fwd = block_table(SECTION_A, -1.0)
    inner_fwd = block_table(SECTION_B, -1.0)
    inner_inv = block_table(SECTION_B, 1.0)
    outer_inv = block_table(SECTION_A, 1.0)
    fwd_cos, fwd_sin = twiddle_pair(SECTION_A, SECTION_B, NCH, -1.0)
    inv_cos, inv_sin = twiddle_pair(SECTION_A, SECTION_B, NCH, 1.0)
    fwd_cos = fwd_cos[:, None, None, :]
    fwd_sin = fwd_sin[:, None, None, :]
    inv_cos = inv_cos[:, None, None, :]
    inv_sin = inv_sin[:, None, None, :]
    local_bins = fan_mask.shape[0]
    fk_gate = (
        fan_mask.reshape(local_bins, SECTION_B, SECTION_A).transpose(2, 0, 1).astype(jnp.float32)
    )
    fk_gate = fk_gate[:, :, None, None, :]
    time_major = record.T
    rim_rows = passed_along(time_major[:HOP], "tm", -1)
    extended = jnp.concatenate([time_major, rim_rows], axis=0)
    blocks = extended.reshape(frames_here + 1, HOP, channels).astype(jnp.float32)
    first_half = (blocks[:-1] * taper[:HOP, None]).astype(jnp.bfloat16)
    second_half = (blocks[1:] * taper[HOP:, None]).astype(jnp.bfloat16)
    spectra = jnp.einsum(
        "jn,fnc->jfc", forward_time[:, :HOP], first_half, preferred_element_type=jnp.float32
    )
    spectra = spectra + jnp.einsum(
        "jn,fnc->jfc", forward_time[:, HOP:], second_half, preferred_element_type=jnp.float32
    )
    spectra = spectra.astype(jnp.bfloat16).reshape(2, BINS, frames_here, channels)
    bin_grid = lax.all_to_all(spectra, "chan", split_axis=1, concat_axis=3, tiled=True)
    bin_count = bin_grid.shape[1]
    item_count = bin_grid.shape[2]
    split_grid = bin_grid.reshape(2, bin_count, item_count, SECTION_A, SECTION_B)
    section_one = jnp.einsum(
        "ipoj,ikfpq->ojkfq", outer_fwd, split_grid, preferred_element_type=jnp.float32
    )
    section_one = rotate(section_one, fwd_cos, fwd_sin).astype(jnp.bfloat16)
    fk_plane = jnp.einsum(
        "ijkfq,iqor->jkfor", section_one, inner_fwd, preferred_element_type=jnp.float32
    )
    fk_plane = (fk_plane * fk_gate).astype(jnp.bfloat16)
    section_three = jnp.einsum(
        "jkfir,iroq->jkfoq", fk_plane, inner_inv, preferred_element_type=jnp.float32
    )
    real_part = section_three[:, :, :, 0]
    imag_part = section_three[:, :, :, 1]
    section_three = jnp.stack(
        [real_part * inv_cos - imag_part * inv_sin, real_part * inv_sin + imag_part * inv_cos]
    ).astype(jnp.bfloat16)
    restored = jnp.einsum(
        "ijkfq,ijop->opkfq", section_three, outer_inv, preferred_element_type=jnp.float32
    )
    restored = (restored * (1.0 / NCH)).astype(jnp.bfloat16)
    restored = restored.transpose(0, 2, 3, 1, 4).reshape(2, bin_count, item_count, NCH)
    returned = lax.all_to_all(restored, "chan", split_axis=3, concat_axis=1, tiled=True)
    signal = jnp.einsum("ikn,ikfc->nfc", inverse_time, returned, preferred_element_type=jnp.float32)
    head_half = signal[:HOP]
    tail_half = signal[HOP:]
    carried = passed_along(tail_half[:, -1].astype(jnp.bfloat16), "tm", 1).astype(jnp.float32)
    output_blocks = head_half + jnp.concatenate([carried[:, None], tail_half[:, :-1]], axis=1)
    return output_blocks.transpose(2, 1, 0).reshape(channels, span_len)


LANES = 128
GROUP = 8
PITCH_Q = SECTION_A + 1
PITCH_J = SECTION_B + 1


def flat_table(order_len, exponent_sign):
    table = block_table(order_len, exponent_sign)
    return table.transpose(2, 3, 0, 1).reshape(2 * order_len, 2 * order_len)


def frame_kernel(
    first, second, taper, fwd_time, inv_time, w_one, w_two, w_three, w_four,
    tw_cos, tw_sin, gate, head, tail, by_q, by_j, restored,
):
    def rows_at(index, size):
        return pl.ds(pl.multiple_of(index * size, size), size)

    def padded(step, g, size):
        return pl.ds(pl.multiple_of(step * (GROUP * (size + 1)), 8) + g * (size + 1), size)

    parts = fwd_time.shape[0]
    for part in range(parts):
        lanes = slice(part * LANES, (part + 1) * LANES)

        @pl.loop(0, SECTION_A // GROUP)
        def _(step):
            rows = rows_at(step, GROUP * SECTION_B)
            left = (first[rows, :].astype(jnp.float32) * taper[:, :HOP]).astype(jnp.bfloat16)
            right = (second[rows, :].astype(jnp.float32) * taper[:, HOP:]).astype(jnp.bfloat16)
            spectra = jnp.dot(left, fwd_time[part, :HOP], preferred_element_type=jnp.float32)
            spectra += jnp.dot(right, fwd_time[part, HOP:], preferred_element_type=jnp.float32)
            for g in range(GROUP):
                for i in range(2):
                    by_q[i, pl.ds(step * GROUP + g, SECTION_B, stride=PITCH_Q), :] = spectra[
                        g * SECTION_B : (g + 1) * SECTION_B, i * LANES : (i + 1) * LANES
                    ]

        @pl.loop(0, SECTION_B // GROUP)
        def _(step):
            columns = []
            for g in range(GROUP):
                rows = padded(step, g, SECTION_A)
                columns.append(
                    jnp.concatenate([by_q[0, rows, :], by_q[1, rows, :]], axis=0).astype(jnp.bfloat16)
                )
            total = jnp.dot(
                w_one[...], jnp.concatenate(columns, axis=1), preferred_element_type=jnp.float32
            )
            for g in range(GROUP):
                rows = rows_at(step * GROUP + g, SECTION_A)
                cosine, sine = tw_cos[rows, :], tw_sin[rows, :]
                real = total[:SECTION_A, g * LANES : (g + 1) * LANES]
                imag = total[SECTION_A:, g * LANES : (g + 1) * LANES]
                spread = pl.ds(step * GROUP + g, SECTION_A, stride=PITCH_J)
                by_j[0, spread, :] = real * cosine + imag * sine
                by_j[1, spread, :] = imag * cosine - real * sine

        @pl.loop(0, SECTION_A // GROUP)
        def _(step):
            columns, gates = [], []
            for g in range(GROUP):
                rows = rows_at(step * GROUP + g, SECTION_B)
                held = padded(step, g, SECTION_B)
                columns.append(
                    jnp.concatenate([by_j[0, held, :], by_j[1, held, :]], axis=0).astype(jnp.bfloat16)
                )
                gates.append(gate[lanes, rows].astype(jnp.float32).T)
            plane = jnp.dot(
                w_two[...], jnp.concatenate(columns, axis=1), preferred_element_type=jnp.float32
            )
            passing = jnp.concatenate(gates, axis=1)
            plane = plane * jnp.concatenate([passing, passing], axis=0)
            total = jnp.dot(
                w_three[...], plane.astype(jnp.bfloat16), preferred_element_type=jnp.float32
            )
            for g in range(GROUP):
                spread = pl.ds(step * GROUP + g, SECTION_B, stride=PITCH_Q)
                for i in range(2):
                    by_q[i, spread, :] = total[
                        i * SECTION_B : (i + 1) * SECTION_B, g * LANES : (g + 1) * LANES
                    ]

        @pl.loop(0, SECTION_B // GROUP)
        def _(step):
            columns = []
            for g in range(GROUP):
                rows = rows_at(step * GROUP + g, SECTION_A)
                cosine, sine = tw_cos[rows, :], tw_sin[rows, :]
                held = padded(step, g, SECTION_A)
                real, imag = by_q[0, held, :], by_q[1, held, :]
                columns.append(
                    jnp.concatenate(
                        [real * cosine - imag * sine, real * sine + imag * cosine], axis=0
                    ).astype(jnp.bfloat16)
                )
            total = jnp.dot(
                w_four[...], jnp.concatenate(columns, axis=1), preferred_element_type=jnp.float32
            ) * (1.0 / NCH)
            for g in range(GROUP):
                spread = pl.ds(step * GROUP + g, SECTION_A, stride=PITCH_J)
                for i in range(2):
                    by_j[i, spread, :] = total[
                        i * SECTION_A : (i + 1) * SECTION_A, g * LANES : (g + 1) * LANES
                    ]

        @pl.loop(0, SECTION_A // GROUP)
        def _(step):
            for i in range(2):
                at = (2 * part + i) * LANES
                for g in range(GROUP):
                    rows = rows_at(step * GROUP + g, SECTION_B)
                    restored[rows, at : at + LANES] = by_j[i, padded(step, g, SECTION_B), :].astype(
                        jnp.bfloat16
                    )

    @pl.loop(0, SECTION_A // GROUP)
    def _(step):
        rows = rows_at(step, GROUP * SECTION_B)
        signal = jnp.dot(restored[rows, :], inv_time[...], preferred_element_type=jnp.float32)
        head[rows, :] = signal[:, :HOP].astype(head.dtype)
        tail[rows, :] = signal[:, HOP:].astype(tail.dtype)


def frame_tables():
    parts = BINS // LANES
    fwd_time = time_table(WIN, BINS).reshape(WIN, 2, parts, LANES)
    fwd_time = fwd_time.transpose(2, 0, 1, 3).reshape(parts, WIN, 2 * LANES)
    inv_time = inverse_time_table(WIN, BINS).reshape(2, parts, LANES, WIN)
    inv_time = inv_time.transpose(1, 0, 2, 3).reshape(2 * BINS, WIN)
    tw_cos, tw_sin = twiddle_pair(SECTION_B, SECTION_A, NCH, 1.0)
    spread = (SECTION_B, SECTION_A, LANES)
    return (
        hann_taper(WIN)[None, :],
        fwd_time,
        inv_time,
        flat_table(SECTION_A, -1.0),
        flat_table(SECTION_B, -1.0),
        flat_table(SECTION_B, 1.0),
        flat_table(SECTION_A, 1.0),
        np.broadcast_to(tw_cos[:, :, None], spread).reshape(NCH, LANES),
        np.broadcast_to(tw_sin[:, :, None], spread).reshape(NCH, LANES),
    )


def filter_frame(first, second, tables, gate):
    half = jax.ShapeDtypeStruct((NCH, HOP), jnp.bfloat16)
    whole = pl.BlockSpec(memory_space=pltpu.VMEM)
    return pl.pallas_call(
        frame_kernel,
        out_shape=(half, half),
        in_specs=[whole] * (3 + len(tables)),
        out_specs=(whole, whole),
        scratch_shapes=[
            pltpu.VMEM((2, SECTION_B * PITCH_Q, LANES), jnp.float32),
            pltpu.VMEM((2, SECTION_A * PITCH_J, LANES), jnp.float32),
            pltpu.VMEM((NCH, 2 * BINS), jnp.bfloat16),
        ],
        compiler_params=pltpu.CompilerParams(vmem_limit_bytes=60 * 1024 * 1024),
        cost_estimate=pl.CostEstimate(
            flops=16_000_000_000, bytes_accessed=30_000_000, transcendentals=0
        ),
    )(first, second, *tables, gate)


def device_at(group, place):
    peers = lax.axis_size("chan")
    place = place + (group % 2) * (peers - 1 - 2 * place)
    if peers % 4 == 0:
        place = place + (place // 4 % 2) * (2 - 4 * (place // 2 % 2))
    return place


def place_of(group, device):
    peers = lax.axis_size("chan")
    if peers % 4 == 0:
        device = device + (device // 4 % 2) * (2 - 4 * (device // 2 % 2))
    return device + (group % 2) * (peers - 1 - 2 * device)


def along_line(group, place, by):
    peers = lax.axis_size("chan")
    spot = group * peers + place + by
    there = spot // peers
    return {"tm": there, "chan": device_at(there, spot % peers)}


def offset_of(step):
    peers = lax.axis_size("chan")
    if peers % 2 == 1:
        return step + 1
    rank = step // 2 + (step % 2) * (peers // 2)
    return peers // 2 + (1 - 2 * (rank % 2)) * ((rank + 1) // 2)


def greet(group, me, place):
    groups, peers = lax.axis_size("tm"), lax.axis_size("chan")
    barrier = pltpu.get_barrier_semaphore()

    def signal(target):
        pl.semaphore_signal(barrier, inc=1, device_id=target, device_id_type=pl.DeviceIdType.MESH)

    @pl.loop(1, peers)
    def _(i):
        signal({"tm": group, "chan": lax.rem(me + i, peers)})

    up = jnp.logical_and(place == 0, group > 0)
    down = jnp.logical_and(place == peers - 1, group < groups - 1)

    @pl.when(up)
    def _():
        signal(along_line(group, place, -1))

    @pl.when(down)
    def _():
        signal(along_line(group, place, 1))

    pl.semaphore_wait(barrier, peers - 1 + up.astype(jnp.int32) + down.astype(jnp.int32))


def remote(source, target, send_sem, recv_sem, device):
    return pltpu.make_async_remote_copy(
        src_ref=source,
        dst_ref=target,
        send_sem=send_sem,
        recv_sem=recv_sem,
        device_id=device,
        device_id_type=pl.DeviceIdType.MESH,
    )


EDGE = 4
WINDOW = 5
AHEAD = 3


def edge_places():
    peers = lax.axis_size("chan")
    return list(range(EDGE, peers, EDGE)) if peers % EDGE == 0 else []


def gather_kernel(record, first, second, nothing, send, recv, pass_send, pass_recv, local, edge_send):
    groups, peers = lax.axis_size("tm"), lax.axis_size("chan")
    group, me = lax.axis_index("tm"), lax.axis_index("chan")
    place = place_of(group, me)
    size = record.shape[0]
    has_prev = jnp.logical_or(place > 0, group > 0)
    has_next = jnp.logical_or(place < peers - 1, group < groups - 1)

    edges = edge_places()
    starts = jnp.logical_and(place > 0, place % EDGE == 0) if edges else place < 0
    ends = jnp.logical_and(place < peers - 1, place % EDGE == EDGE - 1) if edges else place < 0
    passes = jnp.logical_and(has_prev, jnp.logical_not(starts))

    def rows(device):
        return pl.ds(pl.multiple_of(device * size, size), size)

    def block_at(spot):
        return record.at[:, pl.ds(pl.multiple_of(spot * HOP, HOP), HOP)]

    def block(device):
        return block_at(place_of(group, device))

    def edged(at, edge, device):
        return remote(
            block_at(edge), second.at[rows(me)], edge_send.at[at], pass_recv.at[me],
            {"tm": group, "chan": device},
        )

    def sent(device):
        return remote(
            block(device), first.at[rows(me)], send.at[device], recv.at[me],
            {"tm": group, "chan": device},
        )

    def arriving(device):
        return remote(
            block(device), first.at[rows(device)], send.at[device], recv.at[device],
            {"tm": group, "chan": device},
        )

    def passed(source, device):
        return remote(
            source, second.at[rows(device)], pass_send.at[device], pass_recv.at[device],
            along_line(group, place, -1),
        )

    greet(group, me, place)
    own = pltpu.make_async_copy(block(me), first.at[rows(me)], local)
    own.start()

    @pl.when(passes)
    def _():
        passed(block(me), me).start()

    @pl.loop(0, peers - 1 + WINDOW)
    def _(i):
        @pl.when(i < peers - 1)
        def _():
            sent(lax.rem(me + offset_of(i), peers)).start()

        for at, edge in enumerate(edges):
            to = device_at(group, edge - 1)
            due = i == (at + 1) * (peers - 1) // (len(edges) + 1)

            @pl.when(jnp.logical_and(due, to != me))
            def _():
                edged(at, edge, to).start()

            @pl.when(jnp.logical_and(due, to == me))
            def _():
                pltpu.make_async_copy(block_at(edge), second.at[rows(me)], edge_send.at[at]).start()

        @pl.when(i >= WINDOW)
        def _():
            away = offset_of(i - WINDOW)
            device = lax.rem(me + peers - away, peers)
            sent(lax.rem(me + away, peers)).wait_send()
            arriving(device).wait_recv()

            @pl.when(passes)
            def _():
                passed(first.at[rows(device)], device).start()

    own.wait()

    @pl.when(passes)
    def _():
        @pl.loop(0, peers)
        def _(i):
            passed(first.at[rows(i)], i).wait_send()

    for at, edge in enumerate(edges):
        to = device_at(group, edge - 1)

        @pl.when(to != me)
        def _():
            edged(at, edge, to).wait_send()

        @pl.when(to == me)
        def _():
            pltpu.make_async_copy(block_at(edge), second.at[rows(me)], edge_send.at[at]).wait()

    @pl.when(has_next)
    def _():
        @pl.loop(1, peers)
        def _(i):
            device = lax.rem(me + i, peers)
            passed(first.at[rows(device)], device).wait_recv()

    @pl.when(jnp.logical_and(has_next, jnp.logical_not(ends)))
    def _():
        passed(first.at[rows(me)], me).wait_recv()

    @pl.when(jnp.logical_not(has_next))
    def _():
        nothing[...] = jnp.zeros_like(nothing)

        @pl.loop(0, peers)
        def _(i):
            fill = pltpu.make_async_copy(nothing, second.at[rows(i)], local)
            fill.start()
            fill.wait()


def scatter_kernel(head, tail, out, carried, total, send, recv, pass_send, pass_recv, local):
    groups, peers = lax.axis_size("tm"), lax.axis_size("chan")
    group, me = lax.axis_index("tm"), lax.axis_index("chan")
    place = place_of(group, me)
    size = out.shape[0]
    has_prev = jnp.logical_or(place > 0, group > 0)
    has_next = jnp.logical_or(place < peers - 1, group < groups - 1)
    after = along_line(group, place, 1)

    def rows(device):
        return pl.ds(pl.multiple_of(device * size, size), size)

    def block(device):
        return out.at[:, pl.ds(pl.multiple_of(place_of(group, device) * HOP, HOP), HOP)]

    def passed(device):
        return remote(
            tail.at[rows(device)], carried.at[rows(device)], pass_send.at[device],
            pass_recv.at[device], after,
        )

    def sent(device):
        return remote(
            total.at[rows(device)], block(me), send.at[device], recv.at[me],
            {"tm": group, "chan": device},
        )

    def arriving(device):
        return remote(
            total.at[rows(device)], block(device), send.at[device], recv.at[device],
            {"tm": group, "chan": device},
        )

    def add(device):
        @pl.when(has_prev)
        def _():
            passed(device).wait_recv()
            total[rows(device), :] = (
                head[rows(device), :].astype(jnp.float32)
                + carried[rows(device), :].astype(jnp.float32)
            ).astype(total.dtype)

        @pl.when(jnp.logical_not(has_prev))
        def _():
            total[rows(device), :] = head[rows(device), :]

    greet(group, me, place)

    own = pltpu.make_async_copy(total.at[rows(me)], block(me), local)

    @pl.loop(0, peers + AHEAD)
    def _(i):
        @pl.when(jnp.logical_and(has_next, i < peers))
        def _():
            passed(lax.rem(after["chan"] + offset_of(i), peers)).start()

        @pl.when(jnp.logical_and(i >= AHEAD, i < peers - 1 + AHEAD))
        def _():
            device = lax.rem(me + offset_of(i - AHEAD), peers)
            add(device)
            sent(device).start()

        @pl.when(jnp.logical_and(i >= AHEAD + WINDOW, i < peers - 1 + AHEAD))
        def _():
            sent(lax.rem(me + offset_of(i - AHEAD - WINDOW), peers)).wait_send()

    add(me)
    own.start()
    own.wait()

    @pl.loop(max(peers - 1 - WINDOW, 0), peers - 1)
    def _(i):
        sent(lax.rem(me + offset_of(i), peers)).wait_send()

    @pl.loop(1, peers)
    def _(i):
        arriving(lax.rem(me + peers - i, peers)).wait_recv()

    @pl.when(has_next)
    def _():
        @pl.loop(0, peers)
        def _(i):
            passed(i).wait_send()


def exchange_scratch():
    peers = lax.axis_size("chan")
    return [pltpu.SemaphoreType.DMA((peers,))] * 4 + [pltpu.SemaphoreType.DMA]


def gather_frames(record):
    anywhere = pl.BlockSpec(memory_space=pl.ANY)
    half = jax.ShapeDtypeStruct((NCH, HOP), record.dtype)
    return pl.pallas_call(
        gather_kernel,
        out_shape=(half, half),
        in_specs=[anywhere],
        out_specs=(anywhere, anywhere),
        scratch_shapes=[pltpu.VMEM((record.shape[0], HOP), record.dtype)] + exchange_scratch()
        + [pltpu.SemaphoreType.DMA((max(len(edge_places()), 1),))],
        compiler_params=pltpu.CompilerParams(
            collective_id=0, has_side_effects=True, vmem_limit_bytes=60 * 1024 * 1024
        ),
        cost_estimate=pl.CostEstimate(flops=0, bytes_accessed=300_000_000, transcendentals=0),
    )(record)


def scatter_frames(head, tail, channels, span_len):
    anywhere = pl.BlockSpec(memory_space=pl.ANY)
    return pl.pallas_call(
        scatter_kernel,
        out_shape=jax.ShapeDtypeStruct((channels, span_len), head.dtype),
        in_specs=[pl.BlockSpec(memory_space=pltpu.VMEM), anywhere],
        out_specs=anywhere,
        scratch_shapes=[pltpu.VMEM((NCH, HOP), head.dtype)] * 2 + exchange_scratch(),
        compiler_params=pltpu.CompilerParams(
            collective_id=1, has_side_effects=True, vmem_limit_bytes=60 * 1024 * 1024
        ),
        cost_estimate=pl.CostEstimate(flops=0, bytes_accessed=300_000_000, transcendentals=0),
    )(head, tail)


def frames_body(record, fan_mask):
    channels, span_len = record.shape
    local_bins = fan_mask.shape[0]
    gate = fan_mask.astype(jnp.bfloat16).reshape(local_bins, SECTION_B, SECTION_A)
    gate = gate.transpose(0, 2, 1).reshape(local_bins, NCH)
    gate = lax.all_gather(gate, "chan", axis=0, tiled=True)
    first, second = gather_frames(record)
    head, tail = filter_frame(first, second, frame_tables(), gate)
    return scatter_frames(head, tail, channels, span_len).astype(jnp.float32)


def body(record, fan_mask):
    if record.shape[1] // HOP == lax.axis_size("chan"):
        return frames_body(record, fan_mask)
    return bins_body(record, fan_mask)


def solution(mesh):
    placed = (P("chan", "tm"), P("chan", None))
    return jax.shard_map(
        body, mesh=mesh, in_specs=placed, out_specs=P("chan", "tm"), check_vma=False
    )
```

```python
import math

import jax
import jax.numpy as jnp
import numpy as np
from jax import lax
from jax.experimental import pallas as pl
from jax.experimental.pallas import tpu as pltpu
from jax.sharding import PartitionSpec as P

NCH = 8192
SECTION_A = 64
WIN = 512
SECTION_B = 128
HOP = 256
BINS = 256


def passed_along(value, axis, by):
    peers = lax.axis_size(axis)
    pairs = [(i, i + by) for i in range(peers) if 0 <= i + by < peers]
    return lax.ppermute(value, axis, pairs)


def hann_taper(length):
    steps = np.arange(length, dtype=jnp.int32).astype(jnp.float32)
    return 0.5 - 0.5 * np.cos(steps * (2.0 * math.pi / length))


def time_table(length, bins):
    rows = np.arange(length, dtype=jnp.int32)[:, None]
    cols = np.arange(bins, dtype=jnp.int32)[None, :]
    phase = (rows * cols % length).astype(jnp.float32) * (2.0 * math.pi / length)
    return np.concatenate([np.cos(phase), -np.sin(phase)], axis=1).astype(jnp.bfloat16)


def inverse_time_table(length, bins):
    rows = np.arange(bins, dtype=jnp.int32)[:, None]
    cols = np.arange(length, dtype=jnp.int32)[None, :]
    phase = (rows * cols % length).astype(jnp.float32) * (2.0 * math.pi / length)
    weight = np.where(rows == 0, 1.0, 2.0).astype(jnp.float32) / length
    return np.stack([weight * np.cos(phase), -weight * np.sin(phase)]).astype(jnp.bfloat16)


def block_table(order_len, exponent_sign):
    rows = np.arange(order_len, dtype=jnp.int32)[:, None]
    cols = np.arange(order_len, dtype=jnp.int32)[None, :]
    phase = (rows * cols % order_len).astype(jnp.float32) * (2.0 * math.pi / order_len)
    cosine = np.cos(phase)
    sine = exponent_sign * np.sin(phase)
    real_row = np.stack([cosine, sine], axis=1)
    imag_row = np.stack([-sine, cosine], axis=1)
    return np.stack([real_row, imag_row], axis=0).astype(jnp.bfloat16)


def twiddle_pair(row_count, col_count, total, exponent_sign):
    rows = np.arange(row_count, dtype=jnp.int32)[:, None]
    cols = np.arange(col_count, dtype=jnp.int32)[None, :]
    phase = (rows * cols % total).astype(jnp.float32) * (2.0 * math.pi / total)
    return (np.cos(phase), exponent_sign * np.sin(phase))


def rotate(values, cosine, sine):
    return jnp.stack([values[0] * cosine - values[1] * sine, values[0] * sine + values[1] * cosine])


def bins_body(record, fan_mask):
    channels, span_len = record.shape
    frames_here = span_len // HOP
    taper = hann_taper(WIN)
    forward_time = time_table(WIN, BINS).T
    inverse_time = inverse_time_table(WIN, BINS)
    outer_fwd = block_table(SECTION_A, -1.0)
    inner_fwd = block_table(SECTION_B, -1.0)
    inner_inv = block_table(SECTION_B, 1.0)
    outer_inv = block_table(SECTION_A, 1.0)
    fwd_cos, fwd_sin = twiddle_pair(SECTION_A, SECTION_B, NCH, -1.0)
    inv_cos, inv_sin = twiddle_pair(SECTION_A, SECTION_B, NCH, 1.0)
    fwd_cos = fwd_cos[:, None, None, :]
    fwd_sin = fwd_sin[:, None, None, :]
    inv_cos = inv_cos[:, None, None, :]
    inv_sin = inv_sin[:, None, None, :]
    local_bins = fan_mask.shape[0]
    fk_gate = (
        fan_mask.reshape(local_bins, SECTION_B, SECTION_A).transpose(2, 0, 1).astype(jnp.float32)
    )
    fk_gate = fk_gate[:, :, None, None, :]
    time_major = record.T
    rim_rows = passed_along(time_major[:HOP], "tm", -1)
    extended = jnp.concatenate([time_major, rim_rows], axis=0)
    blocks = extended.reshape(frames_here + 1, HOP, channels).astype(jnp.float32)
    first_half = (blocks[:-1] * taper[:HOP, None]).astype(jnp.bfloat16)
    second_half = (blocks[1:] * taper[HOP:, None]).astype(jnp.bfloat16)
    spectra = jnp.einsum(
        "jn,fnc->jfc", forward_time[:, :HOP], first_half, preferred_element_type=jnp.float32
    )
    spectra = spectra + jnp.einsum(
        "jn,fnc->jfc", forward_time[:, HOP:], second_half, preferred_element_type=jnp.float32
    )
    spectra = spectra.astype(jnp.bfloat16).reshape(2, BINS, frames_here, channels)
    bin_grid = lax.all_to_all(spectra, "chan", split_axis=1, concat_axis=3, tiled=True)
    bin_count = bin_grid.shape[1]
    item_count = bin_grid.shape[2]
    split_grid = bin_grid.reshape(2, bin_count, item_count, SECTION_A, SECTION_B)
    section_one = jnp.einsum(
        "ipoj,ikfpq->ojkfq", outer_fwd, split_grid, preferred_element_type=jnp.float32
    )
    section_one = rotate(section_one, fwd_cos, fwd_sin).astype(jnp.bfloat16)
    fk_plane = jnp.einsum(
        "ijkfq,iqor->jkfor", section_one, inner_fwd, preferred_element_type=jnp.float32
    )
    fk_plane = (fk_plane * fk_gate).astype(jnp.bfloat16)
    section_three = jnp.einsum(
        "jkfir,iroq->jkfoq", fk_plane, inner_inv, preferred_element_type=jnp.float32
    )
    real_part = section_three[:, :, :, 0]
    imag_part = section_three[:, :, :, 1]
    section_three = jnp.stack(
        [real_part * inv_cos - imag_part * inv_sin, real_part * inv_sin + imag_part * inv_cos]
    ).astype(jnp.bfloat16)
    restored = jnp.einsum(
        "ijkfq,ijop->opkfq", section_three, outer_inv, preferred_element_type=jnp.float32
    )
    restored = (restored * (1.0 / NCH)).astype(jnp.bfloat16)
    restored = restored.transpose(0, 2, 3, 1, 4).reshape(2, bin_count, item_count, NCH)
    returned = lax.all_to_all(restored, "chan", split_axis=3, concat_axis=1, tiled=True)
    signal = jnp.einsum("ikn,ikfc->nfc", inverse_time, returned, preferred_element_type=jnp.float32)
    head_half = signal[:HOP]
    tail_half = signal[HOP:]
    carried = passed_along(tail_half[:, -1].astype(jnp.bfloat16), "tm", 1).astype(jnp.float32)
    output_blocks = head_half + jnp.concatenate([carried[:, None], tail_half[:, :-1]], axis=1)
    return output_blocks.transpose(2, 1, 0).reshape(channels, span_len)


LANES = 128
GROUP = 8
PITCH_Q = SECTION_A + 1
PITCH_J = SECTION_B + 1


def flat_table(order_len, exponent_sign):
    table = block_table(order_len, exponent_sign)
    return table.transpose(2, 3, 0, 1).reshape(2 * order_len, 2 * order_len)


def frame_kernel(
    first, second, taper, fwd_time, inv_time, w_one, w_two, w_three, w_four,
    tw_cos, tw_sin, gate, head, tail, by_q, by_j, restored,
):
    def rows_at(index, size):
        return pl.ds(pl.multiple_of(index * size, size), size)

    def padded(step, g, size):
        return pl.ds(pl.multiple_of(step * (GROUP * (size + 1)), 8) + g * (size + 1), size)

    parts = fwd_time.shape[0]
    for part in range(parts):
        lanes = slice(part * LANES, (part + 1) * LANES)

        @pl.loop(0, SECTION_A // GROUP)
        def _(step):
            rows = rows_at(step, GROUP * SECTION_B)
            left = (first[rows, :].astype(jnp.float32) * taper[:, :HOP]).astype(jnp.bfloat16)
            right = (second[rows, :].astype(jnp.float32) * taper[:, HOP:]).astype(jnp.bfloat16)
            spectra = jnp.dot(left, fwd_time[part, :HOP], preferred_element_type=jnp.float32)
            spectra += jnp.dot(right, fwd_time[part, HOP:], preferred_element_type=jnp.float32)
            for g in range(GROUP):
                for i in range(2):
                    by_q[i, pl.ds(step * GROUP + g, SECTION_B, stride=PITCH_Q), :] = spectra[
                        g * SECTION_B : (g + 1) * SECTION_B, i * LANES : (i + 1) * LANES
                    ]

        @pl.loop(0, SECTION_B // GROUP)
        def _(step):
            columns = []
            for g in range(GROUP):
                rows = padded(step, g, SECTION_A)
                columns.append(
                    jnp.concatenate([by_q[0, rows, :], by_q[1, rows, :]], axis=0).astype(jnp.bfloat16)
                )
            total = jnp.dot(
                w_one[...], jnp.concatenate(columns, axis=1), preferred_element_type=jnp.float32
            )
            for g in range(GROUP):
                rows = rows_at(step * GROUP + g, SECTION_A)
                cosine, sine = tw_cos[rows, :], tw_sin[rows, :]
                real = total[:SECTION_A, g * LANES : (g + 1) * LANES]
                imag = total[SECTION_A:, g * LANES : (g + 1) * LANES]
                spread = pl.ds(step * GROUP + g, SECTION_A, stride=PITCH_J)
                by_j[0, spread, :] = real * cosine + imag * sine
                by_j[1, spread, :] = imag * cosine - real * sine

        @pl.loop(0, SECTION_A // GROUP)
        def _(step):
            columns, gates = [], []
            for g in range(GROUP):
                rows = rows_at(step * GROUP + g, SECTION_B)
                held = padded(step, g, SECTION_B)
                columns.append(
                    jnp.concatenate([by_j[0, held, :], by_j[1, held, :]], axis=0).astype(jnp.bfloat16)
                )
                gates.append(gate[lanes, rows].astype(jnp.float32).T)
            plane = jnp.dot(
                w_two[...], jnp.concatenate(columns, axis=1), preferred_element_type=jnp.float32
            )
            passing = jnp.concatenate(gates, axis=1)
            plane = plane * jnp.concatenate([passing, passing], axis=0)
            total = jnp.dot(
                w_three[...], plane.astype(jnp.bfloat16), preferred_element_type=jnp.float32
            )
            for g in range(GROUP):
                spread = pl.ds(step * GROUP + g, SECTION_B, stride=PITCH_Q)
                for i in range(2):
                    by_q[i, spread, :] = total[
                        i * SECTION_B : (i + 1) * SECTION_B, g * LANES : (g + 1) * LANES
                    ]

        @pl.loop(0, SECTION_B // GROUP)
        def _(step):
            columns = []
            for g in range(GROUP):
                rows = rows_at(step * GROUP + g, SECTION_A)
                cosine, sine = tw_cos[rows, :], tw_sin[rows, :]
                held = padded(step, g, SECTION_A)
                real, imag = by_q[0, held, :], by_q[1, held, :]
                columns.append(
                    jnp.concatenate(
                        [real * cosine - imag * sine, real * sine + imag * cosine], axis=0
                    ).astype(jnp.bfloat16)
                )
            total = jnp.dot(
                w_four[...], jnp.concatenate(columns, axis=1), preferred_element_type=jnp.float32
            ) * (1.0 / NCH)
            for g in range(GROUP):
                spread = pl.ds(step * GROUP + g, SECTION_A, stride=PITCH_J)
                for i in range(2):
                    by_j[i, spread, :] = total[
                        i * SECTION_A : (i + 1) * SECTION_A, g * LANES : (g + 1) * LANES
                    ]

        @pl.loop(0, SECTION_A // GROUP)
        def _(step):
            for i in range(2):
                at = (2 * part + i) * LANES
                for g in range(GROUP):
                    rows = rows_at(step * GROUP + g, SECTION_B)
                    restored[rows, at : at + LANES] = by_j[i, padded(step, g, SECTION_B), :].astype(
                        jnp.bfloat16
                    )

    @pl.loop(0, SECTION_A // GROUP)
    def _(step):
        rows = rows_at(step, GROUP * SECTION_B)
        signal = jnp.dot(restored[rows, :], inv_time[...], preferred_element_type=jnp.float32)
        head[rows, :] = signal[:, :HOP].astype(head.dtype)
        tail[rows, :] = signal[:, HOP:].astype(tail.dtype)


def frame_tables():
    parts = BINS // LANES
    fwd_time = time_table(WIN, BINS).reshape(WIN, 2, parts, LANES)
    fwd_time = fwd_time.transpose(2, 0, 1, 3).reshape(parts, WIN, 2 * LANES)
    inv_time = inverse_time_table(WIN, BINS).reshape(2, parts, LANES, WIN)
    inv_time = inv_time.transpose(1, 0, 2, 3).reshape(2 * BINS, WIN)
    tw_cos, tw_sin = twiddle_pair(SECTION_B, SECTION_A, NCH, 1.0)
    spread = (SECTION_B, SECTION_A, LANES)
    return (
        hann_taper(WIN)[None, :],
        fwd_time,
        inv_time,
        flat_table(SECTION_A, -1.0),
        flat_table(SECTION_B, -1.0),
        flat_table(SECTION_B, 1.0),
        flat_table(SECTION_A, 1.0),
        np.broadcast_to(tw_cos[:, :, None], spread).reshape(NCH, LANES),
        np.broadcast_to(tw_sin[:, :, None], spread).reshape(NCH, LANES),
    )


def filter_frame(first, second, tables, gate):
    half = jax.ShapeDtypeStruct((NCH, HOP), jnp.bfloat16)
    whole = pl.BlockSpec(memory_space=pltpu.VMEM)
    return pl.pallas_call(
        frame_kernel,
        out_shape=(half, half),
        in_specs=[whole] * (3 + len(tables)),
        out_specs=(whole, whole),
        scratch_shapes=[
            pltpu.VMEM((2, SECTION_B * PITCH_Q, LANES), jnp.float32),
            pltpu.VMEM((2, SECTION_A * PITCH_J, LANES), jnp.float32),
            pltpu.VMEM((NCH, 2 * BINS), jnp.bfloat16),
        ],
        compiler_params=pltpu.CompilerParams(vmem_limit_bytes=60 * 1024 * 1024),
        cost_estimate=pl.CostEstimate(
            flops=16_000_000_000, bytes_accessed=30_000_000, transcendentals=0
        ),
    )(first, second, *tables, gate)


def device_at(group, place):
    peers = lax.axis_size("chan")
    place = place + (group % 2) * (peers - 1 - 2 * place)
    if peers % 4 == 0:
        place = place + (place // 4 % 2) * (2 - 4 * (place // 2 % 2))
    return place


def place_of(group, device):
    peers = lax.axis_size("chan")
    if peers % 4 == 0:
        device = device + (device // 4 % 2) * (2 - 4 * (device // 2 % 2))
    return device + (group % 2) * (peers - 1 - 2 * device)


def along_line(group, place, by):
    peers = lax.axis_size("chan")
    spot = group * peers + place + by
    there = spot // peers
    return {"tm": there, "chan": device_at(there, spot % peers)}


def offset_of(step):
    peers = lax.axis_size("chan")
    if peers % 2 == 1:
        return step + 1
    rank = step // 2 + (step % 2) * (peers // 2)
    return peers // 2 + (1 - 2 * (rank % 2)) * ((rank + 1) // 2)


def greet(group, me, place):
    groups, peers = lax.axis_size("tm"), lax.axis_size("chan")
    barrier = pltpu.get_barrier_semaphore()

    def signal(target):
        pl.semaphore_signal(barrier, inc=1, device_id=target, device_id_type=pl.DeviceIdType.MESH)

    @pl.loop(1, peers)
    def _(i):
        signal({"tm": group, "chan": lax.rem(me + i, peers)})

    up = jnp.logical_and(place == 0, group > 0)
    down = jnp.logical_and(place == peers - 1, group < groups - 1)

    @pl.when(up)
    def _():
        signal(along_line(group, place, -1))

    @pl.when(down)
    def _():
        signal(along_line(group, place, 1))

    pl.semaphore_wait(barrier, peers - 1 + up.astype(jnp.int32) + down.astype(jnp.int32))


def remote(source, target, send_sem, recv_sem, device):
    return pltpu.make_async_remote_copy(
        src_ref=source,
        dst_ref=target,
        send_sem=send_sem,
        recv_sem=recv_sem,
        device_id=device,
        device_id_type=pl.DeviceIdType.MESH,
    )


EDGE = 4
WINDOW = 8
AHEAD = 4


def edge_places():
    peers = lax.axis_size("chan")
    return list(range(EDGE, peers, EDGE)) if peers % EDGE == 0 else []


def gather_kernel(record, first, second, nothing, send, recv, pass_send, pass_recv, local, edge_send):
    groups, peers = lax.axis_size("tm"), lax.axis_size("chan")
    group, me = lax.axis_index("tm"), lax.axis_index("chan")
    place = place_of(group, me)
    size = record.shape[1]
    has_prev = jnp.logical_or(place > 0, group > 0)
    has_next = jnp.logical_or(place < peers - 1, group < groups - 1)

    edges = edge_places()
    starts = jnp.logical_and(place > 0, place % EDGE == 0) if edges else place < 0
    ends = jnp.logical_and(place < peers - 1, place % EDGE == EDGE - 1) if edges else place < 0
    passes = jnp.logical_and(has_prev, jnp.logical_not(starts))

    def rows(device):
        return pl.ds(pl.multiple_of(device * size, size), size)

    def block_at(spot):
        return record.at[spot]

    def block(device):
        return block_at(place_of(group, device))

    def edged(at, edge, device):
        return remote(
            block_at(edge), second.at[rows(me)], edge_send.at[at], pass_recv.at[me],
            {"tm": group, "chan": device},
        )

    def sent(device):
        return remote(
            block(device), first.at[rows(me)], send.at[device], recv.at[me],
            {"tm": group, "chan": device},
        )

    def arriving(device):
        return remote(
            block(device), first.at[rows(device)], send.at[device], recv.at[device],
            {"tm": group, "chan": device},
        )

    def passed(source, device):
        return remote(
            source, second.at[rows(device)], pass_send.at[device], pass_recv.at[device],
            along_line(group, place, -1),
        )

    greet(group, me, place)
    own = pltpu.make_async_copy(block(me), first.at[rows(me)], local)
    own.start()

    @pl.when(passes)
    def _():
        passed(block(me), me).start()

    @pl.loop(0, peers - 1 + WINDOW)
    def _(i):
        @pl.when(i < peers - 1)
        def _():
            sent(lax.rem(me + offset_of(i), peers)).start()

        for at, edge in enumerate(edges):
            to = device_at(group, edge - 1)
            due = i == (at + 1) * (peers - 1) // (len(edges) + 1)

            @pl.when(jnp.logical_and(due, to != me))
            def _():
                edged(at, edge, to).start()

            @pl.when(jnp.logical_and(due, to == me))
            def _():
                pltpu.make_async_copy(block_at(edge), second.at[rows(me)], edge_send.at[at]).start()

        @pl.when(i >= WINDOW)
        def _():
            away = offset_of(i - WINDOW)
            device = lax.rem(me + peers - away, peers)
            sent(lax.rem(me + away, peers)).wait_send()
            arriving(device).wait_recv()

            @pl.when(passes)
            def _():
                passed(first.at[rows(device)], device).start()

    own.wait()

    @pl.when(passes)
    def _():
        @pl.loop(0, peers)
        def _(i):
            passed(first.at[rows(i)], i).wait_send()

    for at, edge in enumerate(edges):
        to = device_at(group, edge - 1)

        @pl.when(to != me)
        def _():
            edged(at, edge, to).wait_send()

        @pl.when(to == me)
        def _():
            pltpu.make_async_copy(block_at(edge), second.at[rows(me)], edge_send.at[at]).wait()

    @pl.when(has_next)
    def _():
        @pl.loop(1, peers)
        def _(i):
            device = lax.rem(me + i, peers)
            passed(first.at[rows(device)], device).wait_recv()

    @pl.when(jnp.logical_and(has_next, jnp.logical_not(ends)))
    def _():
        passed(first.at[rows(me)], me).wait_recv()

    @pl.when(jnp.logical_not(has_next))
    def _():
        nothing[...] = jnp.zeros_like(nothing)

        @pl.loop(0, peers)
        def _(i):
            fill = pltpu.make_async_copy(nothing, second.at[rows(i)], local)
            fill.start()
            fill.wait()


def scatter_kernel(head, tail, out, carried, total, send, recv, pass_send, pass_recv, local):
    groups, peers = lax.axis_size("tm"), lax.axis_size("chan")
    group, me = lax.axis_index("tm"), lax.axis_index("chan")
    place = place_of(group, me)
    size = out.shape[1]
    has_prev = jnp.logical_or(place > 0, group > 0)
    has_next = jnp.logical_or(place < peers - 1, group < groups - 1)
    after = along_line(group, place, 1)

    def rows(device):
        return pl.ds(pl.multiple_of(device * size, size), size)

    def block(device):
        return out.at[place_of(group, device)]

    def passed(device):
        return remote(
            tail.at[rows(device)], carried.at[rows(device)], pass_send.at[device],
            pass_recv.at[device], after,
        )

    def sent(device):
        return remote(
            total.at[rows(device)], block(me), send.at[device], recv.at[me],
            {"tm": group, "chan": device},
        )

    def arriving(device):
        return remote(
            total.at[rows(device)], block(device), send.at[device], recv.at[device],
            {"tm": group, "chan": device},
        )

    def add(device):
        @pl.when(has_prev)
        def _():
            passed(device).wait_recv()
            total[rows(device), :] = (
                head[rows(device), :].astype(jnp.float32)
                + carried[rows(device), :].astype(jnp.float32)
            ).astype(total.dtype)

        @pl.when(jnp.logical_not(has_prev))
        def _():
            total[rows(device), :] = head[rows(device), :]

    greet(group, me, place)

    own = pltpu.make_async_copy(total.at[rows(me)], block(me), local)

    @pl.loop(0, peers + AHEAD)
    def _(i):
        @pl.when(jnp.logical_and(has_next, i < peers))
        def _():
            passed(lax.rem(after["chan"] + offset_of(i), peers)).start()

        @pl.when(jnp.logical_and(i >= AHEAD, i < peers - 1 + AHEAD))
        def _():
            device = lax.rem(me + offset_of(i - AHEAD), peers)
            add(device)
            sent(device).start()

        @pl.when(jnp.logical_and(i >= AHEAD + WINDOW, i < peers - 1 + AHEAD))
        def _():
            sent(lax.rem(me + offset_of(i - AHEAD - WINDOW), peers)).wait_send()

    add(me)
    own.start()
    own.wait()

    @pl.loop(max(peers - 1 - WINDOW, 0), peers - 1)
    def _(i):
        sent(lax.rem(me + offset_of(i), peers)).wait_send()

    @pl.loop(1, peers)
    def _(i):
        arriving(lax.rem(me + peers - i, peers)).wait_recv()

    @pl.when(has_next)
    def _():
        @pl.loop(0, peers)
        def _(i):
            passed(i).wait_send()


def exchange_scratch():
    peers = lax.axis_size("chan")
    return [pltpu.SemaphoreType.DMA((peers,))] * 4 + [pltpu.SemaphoreType.DMA]


def gather_frames(record):
    anywhere = pl.BlockSpec(memory_space=pl.ANY)
    half = jax.ShapeDtypeStruct((NCH, HOP), record.dtype)
    return pl.pallas_call(
        gather_kernel,
        out_shape=(half, half),
        in_specs=[anywhere],
        out_specs=(anywhere, anywhere),
        scratch_shapes=[pltpu.VMEM(record.shape[1:], record.dtype)] + exchange_scratch()
        + [pltpu.SemaphoreType.DMA((max(len(edge_places()), 1),))],
        compiler_params=pltpu.CompilerParams(
            collective_id=0, has_side_effects=True, vmem_limit_bytes=60 * 1024 * 1024
        ),
        cost_estimate=pl.CostEstimate(flops=0, bytes_accessed=300_000_000, transcendentals=0),
    )(record)


def scatter_frames(head, tail, channels):
    peers = lax.axis_size("chan")
    anywhere = pl.BlockSpec(memory_space=pl.ANY)
    return pl.pallas_call(
        scatter_kernel,
        out_shape=jax.ShapeDtypeStruct((peers, channels, HOP), head.dtype),
        in_specs=[pl.BlockSpec(memory_space=pltpu.VMEM), anywhere],
        out_specs=anywhere,
        scratch_shapes=[pltpu.VMEM((NCH, HOP), head.dtype)] * 2 + exchange_scratch(),
        compiler_params=pltpu.CompilerParams(
            collective_id=1, has_side_effects=True, vmem_limit_bytes=60 * 1024 * 1024
        ),
        cost_estimate=pl.CostEstimate(flops=0, bytes_accessed=300_000_000, transcendentals=0),
    )(head, tail)


def frames_body(record, fan_mask):
    channels, span_len = record.shape
    local_bins = fan_mask.shape[0]
    gate = fan_mask.astype(jnp.bfloat16).reshape(local_bins, SECTION_B, SECTION_A)
    gate = gate.transpose(0, 2, 1).reshape(local_bins, NCH)
    gate = lax.all_gather(gate, "chan", axis=0, tiled=True)
    pieces = record.reshape(channels, span_len // HOP, HOP).transpose(1, 0, 2)
    first, second = gather_frames(pieces)
    head, tail = filter_frame(first, second, frame_tables(), gate)
    pieces = scatter_frames(head, tail, channels).astype(jnp.float32)
    return pieces.transpose(1, 0, 2).reshape(channels, span_len)


def body(record, fan_mask):
    if record.shape[1] // HOP == lax.axis_size("chan"):
        return frames_body(record, fan_mask)
    return bins_body(record, fan_mask)


def solution(mesh):
    placed = (P("chan", "tm"), P("chan", None))
    return jax.shard_map(
        body, mesh=mesh, in_specs=placed, out_specs=P("chan", "tm"), check_vma=False
    )
```

```python
import math

import jax
import jax.numpy as jnp
import numpy as np
from jax import lax
from jax.experimental import pallas as pl
from jax.experimental.pallas import tpu as pltpu
from jax.sharding import PartitionSpec as P

NCH = 8192
SECTION_A = 64
WIN = 512
SECTION_B = 128
HOP = 256
BINS = 256


def passed_along(value, axis, by):
    peers = lax.axis_size(axis)
    pairs = [(i, i + by) for i in range(peers) if 0 <= i + by < peers]
    return lax.ppermute(value, axis, pairs)


def hann_taper(length):
    steps = np.arange(length, dtype=jnp.int32).astype(jnp.float32)
    return 0.5 - 0.5 * np.cos(steps * (2.0 * math.pi / length))


def time_table(length, bins):
    rows = np.arange(length, dtype=jnp.int32)[:, None]
    cols = np.arange(bins, dtype=jnp.int32)[None, :]
    phase = (rows * cols % length).astype(jnp.float32) * (2.0 * math.pi / length)
    return np.concatenate([np.cos(phase), -np.sin(phase)], axis=1).astype(jnp.bfloat16)


def inverse_time_table(length, bins):
    rows = np.arange(bins, dtype=jnp.int32)[:, None]
    cols = np.arange(length, dtype=jnp.int32)[None, :]
    phase = (rows * cols % length).astype(jnp.float32) * (2.0 * math.pi / length)
    weight = np.where(rows == 0, 1.0, 2.0).astype(jnp.float32) / length
    return np.stack([weight * np.cos(phase), -weight * np.sin(phase)]).astype(jnp.bfloat16)


def block_table(order_len, exponent_sign):
    rows = np.arange(order_len, dtype=jnp.int32)[:, None]
    cols = np.arange(order_len, dtype=jnp.int32)[None, :]
    phase = (rows * cols % order_len).astype(jnp.float32) * (2.0 * math.pi / order_len)
    cosine = np.cos(phase)
    sine = exponent_sign * np.sin(phase)
    real_row = np.stack([cosine, sine], axis=1)
    imag_row = np.stack([-sine, cosine], axis=1)
    return np.stack([real_row, imag_row], axis=0).astype(jnp.bfloat16)


def twiddle_pair(row_count, col_count, total, exponent_sign):
    rows = np.arange(row_count, dtype=jnp.int32)[:, None]
    cols = np.arange(col_count, dtype=jnp.int32)[None, :]
    phase = (rows * cols % total).astype(jnp.float32) * (2.0 * math.pi / total)
    return (np.cos(phase), exponent_sign * np.sin(phase))


def rotate(values, cosine, sine):
    return jnp.stack([values[0] * cosine - values[1] * sine, values[0] * sine + values[1] * cosine])


def bins_body(record, fan_mask):
    channels, span_len = record.shape
    frames_here = span_len // HOP
    taper = hann_taper(WIN)
    forward_time = time_table(WIN, BINS).T
    inverse_time = inverse_time_table(WIN, BINS)
    outer_fwd = block_table(SECTION_A, -1.0)
    inner_fwd = block_table(SECTION_B, -1.0)
    inner_inv = block_table(SECTION_B, 1.0)
    outer_inv = block_table(SECTION_A, 1.0)
    fwd_cos, fwd_sin = twiddle_pair(SECTION_A, SECTION_B, NCH, -1.0)
    inv_cos, inv_sin = twiddle_pair(SECTION_A, SECTION_B, NCH, 1.0)
    fwd_cos = fwd_cos[:, None, None, :]
    fwd_sin = fwd_sin[:, None, None, :]
    inv_cos = inv_cos[:, None, None, :]
    inv_sin = inv_sin[:, None, None, :]
    local_bins = fan_mask.shape[0]
    fk_gate = (
        fan_mask.reshape(local_bins, SECTION_B, SECTION_A).transpose(2, 0, 1).astype(jnp.float32)
    )
    fk_gate = fk_gate[:, :, None, None, :]
    time_major = record.T
    rim_rows = passed_along(time_major[:HOP], "tm", -1)
    extended = jnp.concatenate([time_major, rim_rows], axis=0)
    blocks = extended.reshape(frames_here + 1, HOP, channels).astype(jnp.float32)
    first_half = (blocks[:-1] * taper[:HOP, None]).astype(jnp.bfloat16)
    second_half = (blocks[1:] * taper[HOP:, None]).astype(jnp.bfloat16)
    spectra = jnp.einsum(
        "jn,fnc->jfc", forward_time[:, :HOP], first_half, preferred_element_type=jnp.float32
    )
    spectra = spectra + jnp.einsum(
        "jn,fnc->jfc", forward_time[:, HOP:], second_half, preferred_element_type=jnp.float32
    )
    spectra = spectra.astype(jnp.bfloat16).reshape(2, BINS, frames_here, channels)
    bin_grid = lax.all_to_all(spectra, "chan", split_axis=1, concat_axis=3, tiled=True)
    bin_count = bin_grid.shape[1]
    item_count = bin_grid.shape[2]
    split_grid = bin_grid.reshape(2, bin_count, item_count, SECTION_A, SECTION_B)
    section_one = jnp.einsum(
        "ipoj,ikfpq->ojkfq", outer_fwd, split_grid, preferred_element_type=jnp.float32
    )
    section_one = rotate(section_one, fwd_cos, fwd_sin).astype(jnp.bfloat16)
    fk_plane = jnp.einsum(
        "ijkfq,iqor->jkfor", section_one, inner_fwd, preferred_element_type=jnp.float32
    )
    fk_plane = (fk_plane * fk_gate).astype(jnp.bfloat16)
    section_three = jnp.einsum(
        "jkfir,iroq->jkfoq", fk_plane, inner_inv, preferred_element_type=jnp.float32
    )
    real_part = section_three[:, :, :, 0]
    imag_part = section_three[:, :, :, 1]
    section_three = jnp.stack(
        [real_part * inv_cos - imag_part * inv_sin, real_part * inv_sin + imag_part * inv_cos]
    ).astype(jnp.bfloat16)
    restored = jnp.einsum(
        "ijkfq,ijop->opkfq", section_three, outer_inv, preferred_element_type=jnp.float32
    )
    restored = (restored * (1.0 / NCH)).astype(jnp.bfloat16)
    restored = restored.transpose(0, 2, 3, 1, 4).reshape(2, bin_count, item_count, NCH)
    returned = lax.all_to_all(restored, "chan", split_axis=3, concat_axis=1, tiled=True)
    signal = jnp.einsum("ikn,ikfc->nfc", inverse_time, returned, preferred_element_type=jnp.float32)
    head_half = signal[:HOP]
    tail_half = signal[HOP:]
    carried = passed_along(tail_half[:, -1].astype(jnp.bfloat16), "tm", 1).astype(jnp.float32)
    output_blocks = head_half + jnp.concatenate([carried[:, None], tail_half[:, :-1]], axis=1)
    return output_blocks.transpose(2, 1, 0).reshape(channels, span_len)


LANES = 128
GROUP = 8
PITCH_Q = SECTION_A + 1
PITCH_J = SECTION_B + 1


def flat_table(order_len, exponent_sign):
    table = block_table(order_len, exponent_sign)
    return table.transpose(2, 3, 0, 1).reshape(2 * order_len, 2 * order_len)


def frame_kernel(
    first, second, taper, fwd_time, inv_time, w_one, w_two, w_three, w_four,
    tw_cos, tw_sin, gate, head, tail, by_q, by_j, restored,
):
    def rows_at(index, size):
        return pl.ds(pl.multiple_of(index * size, size), size)

    def padded(step, g, size):
        return pl.ds(pl.multiple_of(step * (GROUP * (size + 1)), 8) + g * (size + 1), size)

    parts = fwd_time.shape[0]
    for part in range(parts):
        lanes = slice(part * LANES, (part + 1) * LANES)

        @pl.loop(0, SECTION_A // GROUP)
        def _(step):
            rows = rows_at(step, GROUP * SECTION_B)
            left = (first[rows, :].astype(jnp.float32) * taper[:, :HOP]).astype(jnp.bfloat16)
            right = (second[rows, :].astype(jnp.float32) * taper[:, HOP:]).astype(jnp.bfloat16)
            spectra = jnp.dot(left, fwd_time[part, :HOP], preferred_element_type=jnp.float32)
            spectra += jnp.dot(right, fwd_time[part, HOP:], preferred_element_type=jnp.float32)
            for g in range(GROUP):
                for i in range(2):
                    by_q[i, pl.ds(step * GROUP + g, SECTION_B, stride=PITCH_Q), :] = spectra[
                        g * SECTION_B : (g + 1) * SECTION_B, i * LANES : (i + 1) * LANES
                    ]

        @pl.loop(0, SECTION_B // GROUP)
        def _(step):
            columns = []
            for g in range(GROUP):
                rows = padded(step, g, SECTION_A)
                columns.append(
                    jnp.concatenate([by_q[0, rows, :], by_q[1, rows, :]], axis=0).astype(jnp.bfloat16)
                )
            total = jnp.dot(
                w_one[...], jnp.concatenate(columns, axis=1), preferred_element_type=jnp.float32
            )
            for g in range(GROUP):
                rows = rows_at(step * GROUP + g, SECTION_A)
                cosine, sine = tw_cos[rows, :], tw_sin[rows, :]
                real = total[:SECTION_A, g * LANES : (g + 1) * LANES]
                imag = total[SECTION_A:, g * LANES : (g + 1) * LANES]
                spread = pl.ds(step * GROUP + g, SECTION_A, stride=PITCH_J)
                by_j[0, spread, :] = real * cosine + imag * sine
                by_j[1, spread, :] = imag * cosine - real * sine

        @pl.loop(0, SECTION_A // GROUP)
        def _(step):
            columns, gates = [], []
            for g in range(GROUP):
                rows = rows_at(step * GROUP + g, SECTION_B)
                held = padded(step, g, SECTION_B)
                columns.append(
                    jnp.concatenate([by_j[0, held, :], by_j[1, held, :]], axis=0).astype(jnp.bfloat16)
                )
                gates.append(gate[lanes, rows].astype(jnp.float32).T)
            plane = jnp.dot(
                w_two[...], jnp.concatenate(columns, axis=1), preferred_element_type=jnp.float32
            )
            passing = jnp.concatenate(gates, axis=1)
            plane = plane * jnp.concatenate([passing, passing], axis=0)
            total = jnp.dot(
                w_three[...], plane.astype(jnp.bfloat16), preferred_element_type=jnp.float32
            )
            for g in range(GROUP):
                spread = pl.ds(step * GROUP + g, SECTION_B, stride=PITCH_Q)
                for i in range(2):
                    by_q[i, spread, :] = total[
                        i * SECTION_B : (i + 1) * SECTION_B, g * LANES : (g + 1) * LANES
                    ]

        @pl.loop(0, SECTION_B // GROUP)
        def _(step):
            columns = []
            for g in range(GROUP):
                rows = rows_at(step * GROUP + g, SECTION_A)
                cosine, sine = tw_cos[rows, :], tw_sin[rows, :]
                held = padded(step, g, SECTION_A)
                real, imag = by_q[0, held, :], by_q[1, held, :]
                columns.append(
                    jnp.concatenate(
                        [real * cosine - imag * sine, real * sine + imag * cosine], axis=0
                    ).astype(jnp.bfloat16)
                )
            total = jnp.dot(
                w_four[...], jnp.concatenate(columns, axis=1), preferred_element_type=jnp.float32
            ) * (1.0 / NCH)
            for g in range(GROUP):
                spread = pl.ds(step * GROUP + g, SECTION_A, stride=PITCH_J)
                for i in range(2):
                    by_j[i, spread, :] = total[
                        i * SECTION_A : (i + 1) * SECTION_A, g * LANES : (g + 1) * LANES
                    ]

        @pl.loop(0, SECTION_A // GROUP)
        def _(step):
            for i in range(2):
                at = (2 * part + i) * LANES
                for g in range(GROUP):
                    rows = rows_at(step * GROUP + g, SECTION_B)
                    restored[rows, at : at + LANES] = by_j[i, padded(step, g, SECTION_B), :].astype(
                        jnp.bfloat16
                    )

    @pl.loop(0, SECTION_A // GROUP)
    def _(step):
        rows = rows_at(step, GROUP * SECTION_B)
        signal = jnp.dot(restored[rows, :], inv_time[...], preferred_element_type=jnp.float32)
        head[rows, :] = signal[:, :HOP].astype(head.dtype)
        tail[rows, :] = signal[:, HOP:].astype(tail.dtype)


def frame_tables():
    parts = BINS // LANES
    fwd_time = time_table(WIN, BINS).reshape(WIN, 2, parts, LANES)
    fwd_time = fwd_time.transpose(2, 0, 1, 3).reshape(parts, WIN, 2 * LANES)
    inv_time = inverse_time_table(WIN, BINS).reshape(2, parts, LANES, WIN)
    inv_time = inv_time.transpose(1, 0, 2, 3).reshape(2 * BINS, WIN)
    tw_cos, tw_sin = twiddle_pair(SECTION_B, SECTION_A, NCH, 1.0)
    spread = (SECTION_B, SECTION_A, LANES)
    return (
        hann_taper(WIN)[None, :],
        fwd_time,
        inv_time,
        flat_table(SECTION_A, -1.0),
        flat_table(SECTION_B, -1.0),
        flat_table(SECTION_B, 1.0),
        flat_table(SECTION_A, 1.0),
        np.broadcast_to(tw_cos[:, :, None], spread).reshape(NCH, LANES),
        np.broadcast_to(tw_sin[:, :, None], spread).reshape(NCH, LANES),
    )


def filter_frame(first, second, tables, gate):
    half = jax.ShapeDtypeStruct((NCH, HOP), jnp.bfloat16)
    whole = pl.BlockSpec(memory_space=pltpu.VMEM)
    return pl.pallas_call(
        frame_kernel,
        out_shape=(half, half),
        in_specs=[whole] * (3 + len(tables)),
        out_specs=(whole, whole),
        scratch_shapes=[
            pltpu.VMEM((2, SECTION_B * PITCH_Q, LANES), jnp.float32),
            pltpu.VMEM((2, SECTION_A * PITCH_J, LANES), jnp.float32),
            pltpu.VMEM((NCH, 2 * BINS), jnp.bfloat16),
        ],
        compiler_params=pltpu.CompilerParams(vmem_limit_bytes=60 * 1024 * 1024),
        cost_estimate=pl.CostEstimate(
            flops=16_000_000_000, bytes_accessed=30_000_000, transcendentals=0
        ),
    )(first, second, *tables, gate)


def device_at(group, place):
    peers = lax.axis_size("chan")
    place = place + (group % 2) * (peers - 1 - 2 * place)
    if peers % 4 == 0:
        place = place + (place // 4 % 2) * (2 - 4 * (place // 2 % 2))
    return place


def place_of(group, device):
    peers = lax.axis_size("chan")
    if peers % 4 == 0:
        device = device + (device // 4 % 2) * (2 - 4 * (device // 2 % 2))
    return device + (group % 2) * (peers - 1 - 2 * device)


def along_line(group, place, by):
    peers = lax.axis_size("chan")
    spot = group * peers + place + by
    there = spot // peers
    return {"tm": there, "chan": device_at(there, spot % peers)}


def offset_of(step):
    peers = lax.axis_size("chan")
    if peers % 2 == 1:
        return step + 1
    return peers // 2 + (1 - 2 * (step % 2)) * ((step + 1) // 2)


def greet(group, me, place):
    groups, peers = lax.axis_size("tm"), lax.axis_size("chan")
    barrier = pltpu.get_barrier_semaphore()

    def signal(target):
        pl.semaphore_signal(barrier, inc=1, device_id=target, device_id_type=pl.DeviceIdType.MESH)

    @pl.loop(1, peers)
    def _(i):
        signal({"tm": group, "chan": lax.rem(me + i, peers)})

    up = jnp.logical_and(place == 0, group > 0)
    down = jnp.logical_and(place == peers - 1, group < groups - 1)

    @pl.when(up)
    def _():
        signal(along_line(group, place, -1))

    @pl.when(down)
    def _():
        signal(along_line(group, place, 1))

    pl.semaphore_wait(barrier, peers - 1 + up.astype(jnp.int32) + down.astype(jnp.int32))


def remote(source, target, send_sem, recv_sem, device):
    return pltpu.make_async_remote_copy(
        src_ref=source,
        dst_ref=target,
        send_sem=send_sem,
        recv_sem=recv_sem,
        device_id=device,
        device_id_type=pl.DeviceIdType.MESH,
    )


EDGE = 2


def edge_places():
    peers = lax.axis_size("chan")
    return list(range(EDGE, peers, EDGE)) if peers % EDGE == 0 else []


def gather_kernel(record, first, second, nothing, send, recv, pass_send, pass_recv, local, edge_send):
    groups, peers = lax.axis_size("tm"), lax.axis_size("chan")
    group, me = lax.axis_index("tm"), lax.axis_index("chan")
    place = place_of(group, me)
    size = record.shape[0]
    has_prev = jnp.logical_or(place > 0, group > 0)
    has_next = jnp.logical_or(place < peers - 1, group < groups - 1)

    edges = edge_places()
    starts = jnp.logical_and(place > 0, place % EDGE == 0) if edges else place < 0
    ends = jnp.logical_and(place < peers - 1, place % EDGE == EDGE - 1) if edges else place < 0
    passes = jnp.logical_and(has_prev, jnp.logical_not(starts))

    def rows(device):
        return pl.ds(pl.multiple_of(device * size, size), size)

    def block_at(spot):
        return record.at[:, pl.ds(pl.multiple_of(spot * HOP, HOP), HOP)]

    def block(device):
        return block_at(place_of(group, device))

    def edged(at, edge, device):
        return remote(
            block_at(edge), second.at[rows(me)], edge_send.at[at], pass_recv.at[me],
            {"tm": group, "chan": device},
        )

    def sent(device):
        return remote(
            block(device), first.at[rows(me)], send.at[device], recv.at[me],
            {"tm": group, "chan": device},
        )

    def arriving(device):
        return remote(
            block(device), first.at[rows(device)], send.at[device], recv.at[device],
            {"tm": group, "chan": device},
        )

    def passed(source, device):
        return remote(
            source, second.at[rows(device)], pass_send.at[device], pass_recv.at[device],
            along_line(group, place, -1),
        )

    greet(group, me, place)
    own = pltpu.make_async_copy(block(me), first.at[rows(me)], local)
    own.start()

    @pl.loop(0, peers - 1)
    def _(i):
        sent(lax.rem(me + offset_of(i), peers)).start()

    for at, edge in enumerate(edges):
        to = device_at(group, edge - 1)

        @pl.when(to != me)
        def _():
            edged(at, edge, to).start()

        @pl.when(to == me)
        def _():
            pltpu.make_async_copy(block_at(edge), second.at[rows(me)], edge_send.at[at]).start()

    @pl.when(passes)
    def _():
        passed(block(me), me).start()

    @pl.loop(0, peers - 1)
    def _(i):
        device = lax.rem(me + peers - offset_of(i), peers)
        arriving(device).wait_recv()

        @pl.when(passes)
        def _():
            passed(first.at[rows(device)], device).start()

    own.wait()

    @pl.loop(1, peers)
    def _(i):
        sent(lax.rem(me + i, peers)).wait_send()

    @pl.when(passes)
    def _():
        @pl.loop(0, peers)
        def _(i):
            passed(first.at[rows(i)], i).wait_send()

    for at, edge in enumerate(edges):
        to = device_at(group, edge - 1)

        @pl.when(to != me)
        def _():
            edged(at, edge, to).wait_send()

        @pl.when(to == me)
        def _():
            pltpu.make_async_copy(block_at(edge), second.at[rows(me)], edge_send.at[at]).wait()

    @pl.when(has_next)
    def _():
        @pl.loop(1, peers)
        def _(i):
            device = lax.rem(me + i, peers)
            passed(first.at[rows(device)], device).wait_recv()

    @pl.when(jnp.logical_and(has_next, jnp.logical_not(ends)))
    def _():
        passed(first.at[rows(me)], me).wait_recv()

    @pl.when(jnp.logical_not(has_next))
    def _():
        nothing[...] = jnp.zeros_like(nothing)

        @pl.loop(0, peers)
        def _(i):
            fill = pltpu.make_async_copy(nothing, second.at[rows(i)], local)
            fill.start()
            fill.wait()


def scatter_kernel(head, tail, out, carried, total, send, recv, pass_send, pass_recv, local):
    groups, peers = lax.axis_size("tm"), lax.axis_size("chan")
    group, me = lax.axis_index("tm"), lax.axis_index("chan")
    place = place_of(group, me)
    size = out.shape[0]
    has_prev = jnp.logical_or(place > 0, group > 0)
    has_next = jnp.logical_or(place < peers - 1, group < groups - 1)
    after = along_line(group, place, 1)

    def rows(device):
        return pl.ds(pl.multiple_of(device * size, size), size)

    def block(device):
        return out.at[:, pl.ds(pl.multiple_of(place_of(group, device) * HOP, HOP), HOP)]

    def passed(device):
        return remote(
            tail.at[rows(device)], carried.at[rows(device)], pass_send.at[device],
            pass_recv.at[device], after,
        )

    def sent(device):
        return remote(
            total.at[rows(device)], block(me), send.at[device], recv.at[me],
            {"tm": group, "chan": device},
        )

    def arriving(device):
        return remote(
            total.at[rows(device)], block(device), send.at[device], recv.at[device],
            {"tm": group, "chan": device},
        )

    def add(device):
        @pl.when(has_prev)
        def _():
            passed(device).wait_recv()
            total[rows(device), :] = (
                head[rows(device), :].astype(jnp.float32)
                + carried[rows(device), :].astype(jnp.float32)
            ).astype(total.dtype)

        @pl.when(jnp.logical_not(has_prev))
        def _():
            total[rows(device), :] = head[rows(device), :]

    greet(group, me, place)

    @pl.when(has_next)
    def _():
        @pl.loop(0, peers - 1)
        def _(i):
            passed(lax.rem(after["chan"] + offset_of(i), peers)).start()

        passed(after["chan"]).start()

    @pl.loop(0, peers - 1)
    def _(i):
        device = lax.rem(me + offset_of(i), peers)
        add(device)
        sent(device).start()

    add(me)
    own = pltpu.make_async_copy(total.at[rows(me)], block(me), local)
    own.start()
    own.wait()

    @pl.loop(1, peers)
    def _(i):
        arriving(lax.rem(me + peers - i, peers)).wait_recv()

    @pl.loop(1, peers)
    def _(i):
        sent(lax.rem(me + i, peers)).wait_send()

    @pl.when(has_next)
    def _():
        @pl.loop(0, peers)
        def _(i):
            passed(i).wait_send()


def exchange_scratch():
    peers = lax.axis_size("chan")
    return [pltpu.SemaphoreType.DMA((peers,))] * 4 + [pltpu.SemaphoreType.DMA]


def gather_frames(record):
    anywhere = pl.BlockSpec(memory_space=pl.ANY)
    half = jax.ShapeDtypeStruct((NCH, HOP), record.dtype)
    return pl.pallas_call(
        gather_kernel,
        out_shape=(half, half),
        in_specs=[anywhere],
        out_specs=(anywhere, anywhere),
        scratch_shapes=[pltpu.VMEM((record.shape[0], HOP), record.dtype)] + exchange_scratch()
        + [pltpu.SemaphoreType.DMA((max(len(edge_places()), 1),))],
        compiler_params=pltpu.CompilerParams(
            collective_id=0, has_side_effects=True, vmem_limit_bytes=60 * 1024 * 1024
        ),
        cost_estimate=pl.CostEstimate(flops=0, bytes_accessed=300_000_000, transcendentals=0),
    )(record)


def scatter_frames(head, tail, channels, span_len):
    anywhere = pl.BlockSpec(memory_space=pl.ANY)
    return pl.pallas_call(
        scatter_kernel,
        out_shape=jax.ShapeDtypeStruct((channels, span_len), head.dtype),
        in_specs=[pl.BlockSpec(memory_space=pltpu.VMEM), anywhere],
        out_specs=anywhere,
        scratch_shapes=[pltpu.VMEM((NCH, HOP), head.dtype)] * 2 + exchange_scratch(),
        compiler_params=pltpu.CompilerParams(
            collective_id=1, has_side_effects=True, vmem_limit_bytes=60 * 1024 * 1024
        ),
        cost_estimate=pl.CostEstimate(flops=0, bytes_accessed=300_000_000, transcendentals=0),
    )(head, tail)


def frames_body(record, fan_mask):
    channels, span_len = record.shape
    local_bins = fan_mask.shape[0]
    gate = fan_mask.astype(jnp.bfloat16).reshape(local_bins, SECTION_B, SECTION_A)
    gate = gate.transpose(0, 2, 1).reshape(local_bins, NCH)
    gate = lax.all_gather(gate, "chan", axis=0, tiled=True)
    first, second = gather_frames(record)
    head, tail = filter_frame(first, second, frame_tables(), gate)
    return scatter_frames(head, tail, channels, span_len).astype(jnp.float32)


def body(record, fan_mask):
    if record.shape[1] // HOP == lax.axis_size("chan"):
        return frames_body(record, fan_mask)
    return bins_body(record, fan_mask)


def solution(mesh):
    placed = (P("chan", "tm"), P("chan", None))
    return jax.shard_map(
        body, mesh=mesh, in_specs=placed, out_specs=P("chan", "tm"), check_vma=False
    )
```

```python
import math

import jax
import jax.numpy as jnp
import numpy as np
from jax import lax
from jax.experimental import pallas as pl
from jax.experimental.pallas import tpu as pltpu
from jax.sharding import PartitionSpec as P

NCH = 8192
SECTION_A = 64
WIN = 512
SECTION_B = 128
HOP = 256
BINS = 256


def passed_along(value, axis, by):
    peers = lax.axis_size(axis)
    pairs = [(i, i + by) for i in range(peers) if 0 <= i + by < peers]
    return lax.ppermute(value, axis, pairs)


def hann_taper(length):
    steps = np.arange(length, dtype=jnp.int32).astype(jnp.float32)
    return 0.5 - 0.5 * np.cos(steps * (2.0 * math.pi / length))


def time_table(length, bins):
    rows = np.arange(length, dtype=jnp.int32)[:, None]
    cols = np.arange(bins, dtype=jnp.int32)[None, :]
    phase = (rows * cols % length).astype(jnp.float32) * (2.0 * math.pi / length)
    return np.concatenate([np.cos(phase), -np.sin(phase)], axis=1).astype(jnp.bfloat16)


def inverse_time_table(length, bins):
    rows = np.arange(bins, dtype=jnp.int32)[:, None]
    cols = np.arange(length, dtype=jnp.int32)[None, :]
    phase = (rows * cols % length).astype(jnp.float32) * (2.0 * math.pi / length)
    weight = np.where(rows == 0, 1.0, 2.0).astype(jnp.float32) / length
    return np.stack([weight * np.cos(phase), -weight * np.sin(phase)]).astype(jnp.bfloat16)


def block_table(order_len, exponent_sign):
    rows = np.arange(order_len, dtype=jnp.int32)[:, None]
    cols = np.arange(order_len, dtype=jnp.int32)[None, :]
    phase = (rows * cols % order_len).astype(jnp.float32) * (2.0 * math.pi / order_len)
    cosine = np.cos(phase)
    sine = exponent_sign * np.sin(phase)
    real_row = np.stack([cosine, sine], axis=1)
    imag_row = np.stack([-sine, cosine], axis=1)
    return np.stack([real_row, imag_row], axis=0).astype(jnp.bfloat16)


def twiddle_pair(row_count, col_count, total, exponent_sign):
    rows = np.arange(row_count, dtype=jnp.int32)[:, None]
    cols = np.arange(col_count, dtype=jnp.int32)[None, :]
    phase = (rows * cols % total).astype(jnp.float32) * (2.0 * math.pi / total)
    return (np.cos(phase), exponent_sign * np.sin(phase))


def rotate(values, cosine, sine):
    return jnp.stack([values[0] * cosine - values[1] * sine, values[0] * sine + values[1] * cosine])


def bins_body(record, fan_mask):
    channels, span_len = record.shape
    frames_here = span_len // HOP
    taper = hann_taper(WIN)
    forward_time = time_table(WIN, BINS).T
    inverse_time = inverse_time_table(WIN, BINS)
    outer_fwd = block_table(SECTION_A, -1.0)
    inner_fwd = block_table(SECTION_B, -1.0)
    inner_inv = block_table(SECTION_B, 1.0)
    outer_inv = block_table(SECTION_A, 1.0)
    fwd_cos, fwd_sin = twiddle_pair(SECTION_A, SECTION_B, NCH, -1.0)
    inv_cos, inv_sin = twiddle_pair(SECTION_A, SECTION_B, NCH, 1.0)
    fwd_cos = fwd_cos[:, None, None, :]
    fwd_sin = fwd_sin[:, None, None, :]
    inv_cos = inv_cos[:, None, None, :]
    inv_sin = inv_sin[:, None, None, :]
    local_bins = fan_mask.shape[0]
    fk_gate = (
        fan_mask.reshape(local_bins, SECTION_B, SECTION_A).transpose(2, 0, 1).astype(jnp.float32)
    )
    fk_gate = fk_gate[:, :, None, None, :]
    time_major = record.T
    rim_rows = passed_along(time_major[:HOP], "tm", -1)
    extended = jnp.concatenate([time_major, rim_rows], axis=0)
    blocks = extended.reshape(frames_here + 1, HOP, channels).astype(jnp.float32)
    first_half = (blocks[:-1] * taper[:HOP, None]).astype(jnp.bfloat16)
    second_half = (blocks[1:] * taper[HOP:, None]).astype(jnp.bfloat16)
    spectra = jnp.einsum(
        "jn,fnc->jfc", forward_time[:, :HOP], first_half, preferred_element_type=jnp.float32
    )
    spectra = spectra + jnp.einsum(
        "jn,fnc->jfc", forward_time[:, HOP:], second_half, preferred_element_type=jnp.float32
    )
    spectra = spectra.astype(jnp.bfloat16).reshape(2, BINS, frames_here, channels)
    bin_grid = lax.all_to_all(spectra, "chan", split_axis=1, concat_axis=3, tiled=True)
    bin_count = bin_grid.shape[1]
    item_count = bin_grid.shape[2]
    split_grid = bin_grid.reshape(2, bin_count, item_count, SECTION_A, SECTION_B)
    section_one = jnp.einsum(
        "ipoj,ikfpq->ojkfq", outer_fwd, split_grid, preferred_element_type=jnp.float32
    )
    section_one = rotate(section_one, fwd_cos, fwd_sin).astype(jnp.bfloat16)
    fk_plane = jnp.einsum(
        "ijkfq,iqor->jkfor", section_one, inner_fwd, preferred_element_type=jnp.float32
    )
    fk_plane = (fk_plane * fk_gate).astype(jnp.bfloat16)
    section_three = jnp.einsum(
        "jkfir,iroq->jkfoq", fk_plane, inner_inv, preferred_element_type=jnp.float32
    )
    real_part = section_three[:, :, :, 0]
    imag_part = section_three[:, :, :, 1]
    section_three = jnp.stack(
        [real_part * inv_cos - imag_part * inv_sin, real_part * inv_sin + imag_part * inv_cos]
    ).astype(jnp.bfloat16)
    restored = jnp.einsum(
        "ijkfq,ijop->opkfq", section_three, outer_inv, preferred_element_type=jnp.float32
    )
    restored = (restored * (1.0 / NCH)).astype(jnp.bfloat16)
    restored = restored.transpose(0, 2, 3, 1, 4).reshape(2, bin_count, item_count, NCH)
    returned = lax.all_to_all(restored, "chan", split_axis=3, concat_axis=1, tiled=True)
    signal = jnp.einsum("ikn,ikfc->nfc", inverse_time, returned, preferred_element_type=jnp.float32)
    head_half = signal[:HOP]
    tail_half = signal[HOP:]
    carried = passed_along(tail_half[:, -1].astype(jnp.bfloat16), "tm", 1).astype(jnp.float32)
    output_blocks = head_half + jnp.concatenate([carried[:, None], tail_half[:, :-1]], axis=1)
    return output_blocks.transpose(2, 1, 0).reshape(channels, span_len)


LANES = 128
GROUP = 8
PITCH_Q = SECTION_A + 1
PITCH_J = SECTION_B + 1


def flat_table(order_len, exponent_sign):
    table = block_table(order_len, exponent_sign)
    return table.transpose(2, 3, 0, 1).reshape(2 * order_len, 2 * order_len)


def frame_kernel(
    first, second, taper, fwd_time, inv_time, w_one, w_two, w_three, w_four,
    tw_cos, tw_sin, gate, head, tail, by_q, by_j, restored,
):
    def rows_at(index, size):
        return pl.ds(pl.multiple_of(index * size, size), size)

    def padded(step, g, size):
        return pl.ds(pl.multiple_of(step * (GROUP * (size + 1)), 8) + g * (size + 1), size)

    parts = fwd_time.shape[0]
    for part in range(parts):
        lanes = slice(part * LANES, (part + 1) * LANES)

        @pl.loop(0, SECTION_A // GROUP)
        def _(step):
            rows = rows_at(step, GROUP * SECTION_B)
            left = (first[rows, :].astype(jnp.float32) * taper[:, :HOP]).astype(jnp.bfloat16)
            right = (second[rows, :].astype(jnp.float32) * taper[:, HOP:]).astype(jnp.bfloat16)
            spectra = jnp.dot(left, fwd_time[part, :HOP], preferred_element_type=jnp.float32)
            spectra += jnp.dot(right, fwd_time[part, HOP:], preferred_element_type=jnp.float32)
            for g in range(GROUP):
                for i in range(2):
                    by_q[i, pl.ds(step * GROUP + g, SECTION_B, stride=PITCH_Q), :] = spectra[
                        g * SECTION_B : (g + 1) * SECTION_B, i * LANES : (i + 1) * LANES
                    ]

        @pl.loop(0, SECTION_B // GROUP)
        def _(step):
            columns = []
            for g in range(GROUP):
                rows = padded(step, g, SECTION_A)
                columns.append(
                    jnp.concatenate([by_q[0, rows, :], by_q[1, rows, :]], axis=0).astype(jnp.bfloat16)
                )
            total = jnp.dot(
                w_one[...], jnp.concatenate(columns, axis=1), preferred_element_type=jnp.float32
            )
            for g in range(GROUP):
                rows = rows_at(step * GROUP + g, SECTION_A)
                cosine, sine = tw_cos[rows, :], tw_sin[rows, :]
                real = total[:SECTION_A, g * LANES : (g + 1) * LANES]
                imag = total[SECTION_A:, g * LANES : (g + 1) * LANES]
                spread = pl.ds(step * GROUP + g, SECTION_A, stride=PITCH_J)
                by_j[0, spread, :] = real * cosine + imag * sine
                by_j[1, spread, :] = imag * cosine - real * sine

        @pl.loop(0, SECTION_A // GROUP)
        def _(step):
            columns, gates = [], []
            for g in range(GROUP):
                rows = rows_at(step * GROUP + g, SECTION_B)
                held = padded(step, g, SECTION_B)
                columns.append(
                    jnp.concatenate([by_j[0, held, :], by_j[1, held, :]], axis=0).astype(jnp.bfloat16)
                )
                gates.append(gate[lanes, rows].astype(jnp.float32).T)
            plane = jnp.dot(
                w_two[...], jnp.concatenate(columns, axis=1), preferred_element_type=jnp.float32
            )
            passing = jnp.concatenate(gates, axis=1)
            plane = plane * jnp.concatenate([passing, passing], axis=0)
            total = jnp.dot(
                w_three[...], plane.astype(jnp.bfloat16), preferred_element_type=jnp.float32
            )
            for g in range(GROUP):
                spread = pl.ds(step * GROUP + g, SECTION_B, stride=PITCH_Q)
                for i in range(2):
                    by_q[i, spread, :] = total[
                        i * SECTION_B : (i + 1) * SECTION_B, g * LANES : (g + 1) * LANES
                    ]

        @pl.loop(0, SECTION_B // GROUP)
        def _(step):
            columns = []
            for g in range(GROUP):
                rows = rows_at(step * GROUP + g, SECTION_A)
                cosine, sine = tw_cos[rows, :], tw_sin[rows, :]
                held = padded(step, g, SECTION_A)
                real, imag = by_q[0, held, :], by_q[1, held, :]
                columns.append(
                    jnp.concatenate(
                        [real * cosine - imag * sine, real * sine + imag * cosine], axis=0
                    ).astype(jnp.bfloat16)
                )
            total = jnp.dot(
                w_four[...], jnp.concatenate(columns, axis=1), preferred_element_type=jnp.float32
            ) * (1.0 / NCH)
            for g in range(GROUP):
                spread = pl.ds(step * GROUP + g, SECTION_A, stride=PITCH_J)
                for i in range(2):
                    by_j[i, spread, :] = total[
                        i * SECTION_A : (i + 1) * SECTION_A, g * LANES : (g + 1) * LANES
                    ]

        @pl.loop(0, SECTION_A // GROUP)
        def _(step):
            for i in range(2):
                at = (2 * part + i) * LANES
                for g in range(GROUP):
                    rows = rows_at(step * GROUP + g, SECTION_B)
                    restored[rows, at : at + LANES] = by_j[i, padded(step, g, SECTION_B), :].astype(
                        jnp.bfloat16
                    )

    @pl.loop(0, SECTION_A // GROUP)
    def _(step):
        rows = rows_at(step, GROUP * SECTION_B)
        signal = jnp.dot(restored[rows, :], inv_time[...], preferred_element_type=jnp.float32)
        head[rows, :] = signal[:, :HOP].astype(head.dtype)
        tail[rows, :] = signal[:, HOP:].astype(tail.dtype)


def frame_tables():
    parts = BINS // LANES
    fwd_time = time_table(WIN, BINS).reshape(WIN, 2, parts, LANES)
    fwd_time = fwd_time.transpose(2, 0, 1, 3).reshape(parts, WIN, 2 * LANES)
    inv_time = inverse_time_table(WIN, BINS).reshape(2, parts, LANES, WIN)
    inv_time = inv_time.transpose(1, 0, 2, 3).reshape(2 * BINS, WIN)
    tw_cos, tw_sin = twiddle_pair(SECTION_B, SECTION_A, NCH, 1.0)
    spread = (SECTION_B, SECTION_A, LANES)
    return (
        hann_taper(WIN)[None, :],
        fwd_time,
        inv_time,
        flat_table(SECTION_A, -1.0),
        flat_table(SECTION_B, -1.0),
        flat_table(SECTION_B, 1.0),
        flat_table(SECTION_A, 1.0),
        np.broadcast_to(tw_cos[:, :, None], spread).reshape(NCH, LANES),
        np.broadcast_to(tw_sin[:, :, None], spread).reshape(NCH, LANES),
    )


def filter_frame(first, second, tables, gate):
    half = jax.ShapeDtypeStruct((NCH, HOP), jnp.bfloat16)
    whole = pl.BlockSpec(memory_space=pltpu.VMEM)
    return pl.pallas_call(
        frame_kernel,
        out_shape=(half, half),
        in_specs=[whole] * (3 + len(tables)),
        out_specs=(whole, whole),
        scratch_shapes=[
            pltpu.VMEM((2, SECTION_B * PITCH_Q, LANES), jnp.float32),
            pltpu.VMEM((2, SECTION_A * PITCH_J, LANES), jnp.float32),
            pltpu.VMEM((NCH, 2 * BINS), jnp.bfloat16),
        ],
        compiler_params=pltpu.CompilerParams(vmem_limit_bytes=60 * 1024 * 1024),
        cost_estimate=pl.CostEstimate(
            flops=16_000_000_000, bytes_accessed=30_000_000, transcendentals=0
        ),
    )(first, second, *tables, gate)


def device_at(group, place):
    peers = lax.axis_size("chan")
    place = place + (group % 2) * (peers - 1 - 2 * place)
    if peers % 4 == 0:
        place = place + (place // 4 % 2) * (2 - 4 * (place // 2 % 2))
    return place


def place_of(group, device):
    peers = lax.axis_size("chan")
    if peers % 4 == 0:
        device = device + (device // 4 % 2) * (2 - 4 * (device // 2 % 2))
    return device + (group % 2) * (peers - 1 - 2 * device)


def along_line(group, place, by):
    peers = lax.axis_size("chan")
    spot = group * peers + place + by
    there = spot // peers
    return {"tm": there, "chan": device_at(there, spot % peers)}


def offset_of(step):
    peers = lax.axis_size("chan")
    if peers % 2 == 1:
        return step + 1
    return peers // 2 + (1 - 2 * (step % 2)) * ((step + 1) // 2)


def greet(group, me, place):
    groups, peers = lax.axis_size("tm"), lax.axis_size("chan")
    barrier = pltpu.get_barrier_semaphore()

    def signal(target):
        pl.semaphore_signal(barrier, inc=1, device_id=target, device_id_type=pl.DeviceIdType.MESH)

    @pl.loop(1, peers)
    def _(i):
        signal({"tm": group, "chan": lax.rem(me + i, peers)})

    up = jnp.logical_and(place == 0, group > 0)
    down = jnp.logical_and(place == peers - 1, group < groups - 1)

    @pl.when(up)
    def _():
        signal(along_line(group, place, -1))

    @pl.when(down)
    def _():
        signal(along_line(group, place, 1))

    pl.semaphore_wait(barrier, peers - 1 + up.astype(jnp.int32) + down.astype(jnp.int32))


def remote(source, target, send_sem, recv_sem, device):
    return pltpu.make_async_remote_copy(
        src_ref=source,
        dst_ref=target,
        send_sem=send_sem,
        recv_sem=recv_sem,
        device_id=device,
        device_id_type=pl.DeviceIdType.MESH,
    )


EDGE = 4
WINDOW = 5
AHEAD = 3


def edge_places():
    peers = lax.axis_size("chan")
    return list(range(EDGE, peers, EDGE)) if peers % EDGE == 0 else []


def gather_kernel(record, first, second, nothing, send, recv, pass_send, pass_recv, local, edge_send):
    groups, peers = lax.axis_size("tm"), lax.axis_size("chan")
    group, me = lax.axis_index("tm"), lax.axis_index("chan")
    place = place_of(group, me)
    size = record.shape[0]
    has_prev = jnp.logical_or(place > 0, group > 0)
    has_next = jnp.logical_or(place < peers - 1, group < groups - 1)

    edges = edge_places()
    starts = jnp.logical_and(place > 0, place % EDGE == 0) if edges else place < 0
    ends = jnp.logical_and(place < peers - 1, place % EDGE == EDGE - 1) if edges else place < 0
    passes = jnp.logical_and(has_prev, jnp.logical_not(starts))

    def rows(device):
        return pl.ds(pl.multiple_of(device * size, size), size)

    def block_at(spot):
        return record.at[:, pl.ds(pl.multiple_of(spot * HOP, HOP), HOP)]

    def block(device):
        return block_at(place_of(group, device))

    def edged(at, edge, device):
        return remote(
            block_at(edge), second.at[rows(me)], edge_send.at[at], pass_recv.at[me],
            {"tm": group, "chan": device},
        )

    def sent(device):
        return remote(
            block(device), first.at[rows(me)], send.at[device], recv.at[me],
            {"tm": group, "chan": device},
        )

    def arriving(device):
        return remote(
            block(device), first.at[rows(device)], send.at[device], recv.at[device],
            {"tm": group, "chan": device},
        )

    def passed(source, device):
        return remote(
            source, second.at[rows(device)], pass_send.at[device], pass_recv.at[device],
            along_line(group, place, -1),
        )

    greet(group, me, place)
    own = pltpu.make_async_copy(block(me), first.at[rows(me)], local)
    own.start()

    @pl.loop(0, peers - 1)
    def _(i):
        sent(lax.rem(me + offset_of(i), peers)).start()

    for at, edge in enumerate(edges):
        to = device_at(group, edge - 1)

        @pl.when(to != me)
        def _():
            edged(at, edge, to).start()

        @pl.when(to == me)
        def _():
            pltpu.make_async_copy(block_at(edge), second.at[rows(me)], edge_send.at[at]).start()

    @pl.when(passes)
    def _():
        passed(block(me), me).start()

    @pl.loop(0, peers - 1)
    def _(i):
        device = lax.rem(me + peers - offset_of(i), peers)
        arriving(device).wait_recv()

        @pl.when(passes)
        def _():
            passed(first.at[rows(device)], device).start()

    own.wait()

    @pl.loop(1, peers)
    def _(i):
        sent(lax.rem(me + i, peers)).wait_send()

    @pl.when(passes)
    def _():
        @pl.loop(0, peers)
        def _(i):
            passed(first.at[rows(i)], i).wait_send()

    for at, edge in enumerate(edges):
        to = device_at(group, edge - 1)

        @pl.when(to != me)
        def _():
            edged(at, edge, to).wait_send()

        @pl.when(to == me)
        def _():
            pltpu.make_async_copy(block_at(edge), second.at[rows(me)], edge_send.at[at]).wait()

    @pl.when(has_next)
    def _():
        @pl.loop(1, peers)
        def _(i):
            device = lax.rem(me + i, peers)
            passed(first.at[rows(device)], device).wait_recv()

    @pl.when(jnp.logical_and(has_next, jnp.logical_not(ends)))
    def _():
        passed(first.at[rows(me)], me).wait_recv()

    @pl.when(jnp.logical_not(has_next))
    def _():
        nothing[...] = jnp.zeros_like(nothing)

        @pl.loop(0, peers)
        def _(i):
            fill = pltpu.make_async_copy(nothing, second.at[rows(i)], local)
            fill.start()
            fill.wait()


def scatter_kernel(head, tail, out, carried, total, send, recv, pass_send, pass_recv, local):
    groups, peers = lax.axis_size("tm"), lax.axis_size("chan")
    group, me = lax.axis_index("tm"), lax.axis_index("chan")
    place = place_of(group, me)
    size = out.shape[0]
    has_prev = jnp.logical_or(place > 0, group > 0)
    has_next = jnp.logical_or(place < peers - 1, group < groups - 1)
    after = along_line(group, place, 1)

    def rows(device):
        return pl.ds(pl.multiple_of(device * size, size), size)

    def block(device):
        return out.at[:, pl.ds(pl.multiple_of(place_of(group, device) * HOP, HOP), HOP)]

    def passed(device):
        return remote(
            tail.at[rows(device)], carried.at[rows(device)], pass_send.at[device],
            pass_recv.at[device], after,
        )

    def sent(device):
        return remote(
            total.at[rows(device)], block(me), send.at[device], recv.at[me],
            {"tm": group, "chan": device},
        )

    def arriving(device):
        return remote(
            total.at[rows(device)], block(device), send.at[device], recv.at[device],
            {"tm": group, "chan": device},
        )

    def add(device):
        @pl.when(has_prev)
        def _():
            passed(device).wait_recv()
            total[rows(device), :] = (
                head[rows(device), :].astype(jnp.float32)
                + carried[rows(device), :].astype(jnp.float32)
            ).astype(total.dtype)

        @pl.when(jnp.logical_not(has_prev))
        def _():
            total[rows(device), :] = head[rows(device), :]

    greet(group, me, place)

    own = pltpu.make_async_copy(total.at[rows(me)], block(me), local)

    @pl.loop(0, peers + AHEAD)
    def _(i):
        @pl.when(jnp.logical_and(has_next, i < peers))
        def _():
            passed(lax.rem(after["chan"] + offset_of(i), peers)).start()

        @pl.when(jnp.logical_and(i >= AHEAD, i < peers - 1 + AHEAD))
        def _():
            device = lax.rem(me + offset_of(i - AHEAD), peers)
            add(device)
            sent(device).start()

        @pl.when(jnp.logical_and(i >= AHEAD + WINDOW, i < peers - 1 + AHEAD))
        def _():
            sent(lax.rem(me + offset_of(i - AHEAD - WINDOW), peers)).wait_send()

    add(me)
    own.start()
    own.wait()

    @pl.loop(max(peers - 1 - WINDOW, 0), peers - 1)
    def _(i):
        sent(lax.rem(me + offset_of(i), peers)).wait_send()

    @pl.loop(1, peers)
    def _(i):
        arriving(lax.rem(me + peers - i, peers)).wait_recv()

    @pl.when(has_next)
    def _():
        @pl.loop(0, peers)
        def _(i):
            passed(i).wait_send()


def exchange_scratch():
    peers = lax.axis_size("chan")
    return [pltpu.SemaphoreType.DMA((peers,))] * 4 + [pltpu.SemaphoreType.DMA]


def gather_frames(record):
    anywhere = pl.BlockSpec(memory_space=pl.ANY)
    half = jax.ShapeDtypeStruct((NCH, HOP), record.dtype)
    return pl.pallas_call(
        gather_kernel,
        out_shape=(half, half),
        in_specs=[anywhere],
        out_specs=(anywhere, anywhere),
        scratch_shapes=[pltpu.VMEM((record.shape[0], HOP), record.dtype)] + exchange_scratch()
        + [pltpu.SemaphoreType.DMA((max(len(edge_places()), 1),))],
        compiler_params=pltpu.CompilerParams(
            collective_id=0, has_side_effects=True, vmem_limit_bytes=60 * 1024 * 1024
        ),
        cost_estimate=pl.CostEstimate(flops=0, bytes_accessed=300_000_000, transcendentals=0),
    )(record)


def scatter_frames(head, tail, channels, span_len):
    anywhere = pl.BlockSpec(memory_space=pl.ANY)
    return pl.pallas_call(
        scatter_kernel,
        out_shape=jax.ShapeDtypeStruct((channels, span_len), head.dtype),
        in_specs=[pl.BlockSpec(memory_space=pltpu.VMEM), anywhere],
        out_specs=anywhere,
        scratch_shapes=[pltpu.VMEM((NCH, HOP), head.dtype)] * 2 + exchange_scratch(),
        compiler_params=pltpu.CompilerParams(
            collective_id=1, has_side_effects=True, vmem_limit_bytes=60 * 1024 * 1024
        ),
        cost_estimate=pl.CostEstimate(flops=0, bytes_accessed=300_000_000, transcendentals=0),
    )(head, tail)


def frames_body(record, fan_mask):
    channels, span_len = record.shape
    local_bins = fan_mask.shape[0]
    gate = fan_mask.astype(jnp.bfloat16).reshape(local_bins, SECTION_B, SECTION_A)
    gate = gate.transpose(0, 2, 1).reshape(local_bins, NCH)
    gate = lax.all_gather(gate, "chan", axis=0, tiled=True)
    first, second = gather_frames(record)
    head, tail = filter_frame(first, second, frame_tables(), gate)
    return scatter_frames(head, tail, channels, span_len).astype(jnp.float32)


def body(record, fan_mask):
    if record.shape[1] // HOP == lax.axis_size("chan"):
        return frames_body(record, fan_mask)
    return bins_body(record, fan_mask)


def solution(mesh):
    placed = (P("chan", "tm"), P("chan", None))
    return jax.shard_map(
        body, mesh=mesh, in_specs=placed, out_specs=P("chan", "tm"), check_vma=False
    )
```
